256 devices in a mesh: seg: 8 (over x, core), blk: 32 (over z, y).
Axes of the slice: x: 4, y: 4, z: 8, core: 2. Of those that a mesh axis runs over, the one named last changes fastest.
Arguments:
- start_vector: bfloat16 [8, 128, 128, 128], P('seg', 'blk'), may hold values from -6 to 6
- left_environment: bfloat16 [8, 128, 34, 128, 128], P('seg', 'blk'), may hold values from -0.5 to 0.5
- right_environment: bfloat16 [8, 128, 34, 128, 128], P('seg', 'blk'), may hold values from -0.5 to 0.5
- block_energy: float32 [8, 128], P('seg', 'blk'), may hold values from -2 to 2
- sector_rows: int32 [8, 128], P('seg', 'blk'), may hold values from 32 to 128, as said below
- sector_cols: int32 [8, 128], P('seg', 'blk'), may hold values from 32 to 128, as said below
- feed_block: int32 [8, 128, 34], P('seg', 'blk'), may hold values from 0 to 128, as said below
Outputs:
- coefficients: float32 [8, 6], P('seg')
- residual: float32 [8, 128, 128, 128], P('seg', 'blk')
The draws below stay inside these ranges and needn't reach their ends.
Inputs may be any that keep to these rules, and one draw needn't show every extreme that they name: `sector_rows`: the first block of every segment fills its tile. `sector_cols`: the first block of every segment fills its tile. `feed_block`: 128 marks an absent channel; absent channels come after the present ones of a block, and the first block of every segment has all 34 channels.
All inputs are finite; a program needn't handle non-finite values.
Results may differ from the reference program's by a relative error of at most 0.014.
Values may be sent and summed in bfloat16 or wider, within the bound.
A program may use at most 128 MiB of HBM per device.

```python
import jax
import jax.numpy as jnp
from jax import lax

TILE = 128
NB_DEV = 4
MW = 34
STEPS = 3
NB = 128
NSEG = 8
N_BLK = 32


def draw_sector_rows(key, part):
    sizes = jax.random.randint(key, (NSEG, NB), TILE // 4, TILE + 1)
    return sizes.at[:, 0].set(TILE).astype(jnp.int32)


def draw_sector_cols(key, part):
    sizes = jax.random.randint(jax.random.fold_in(key, 7), (NSEG, NB), TILE // 4, TILE + 1)
    return sizes.at[:, 0].set(TILE).astype(jnp.int32)


def draw_feed_block(key, part):
    first_key, second_key = jax.random.split(jax.random.fold_in(key, 11))
    present = jax.random.randint(first_key, (NSEG, NB, 1), 3 * MW // 4, MW + 1)
    present = present.at[:, 0, :].set(MW)
    goals = jax.random.randint(second_key, (NSEG, NB, MW), 0, NB)
    channel = jnp.arange(MW, dtype=jnp.int32)
    return jnp.where(channel[None, None, :] < present, goals, NB).astype(jnp.int32)


def block_levels(own_key, dims, cuts, low, top_value):
    level, own = 1.0, jax.random.fold_in(own_key, 6)
    for axis_at, blocks in cuts:
        steps = jnp.exp(jax.random.uniform(jax.random.fold_in(own, axis_at), (blocks,), jnp.float32, low / len(cuts), top_value / len(cuts)))
        level = level * jnp.repeat(steps, dims[axis_at] // blocks).reshape([-1 if axis == axis_at else 1 for axis in range(len(dims))])
    return level


def bell_draw(key, dims, deviation, reach, shards=(), kind=jnp.bfloat16):
    loudness = block_levels(key, dims, shards, -0.22, 0.18) if shards else 1.0
    drawn = jax.random.normal(key, dims, jnp.float32) * deviation * loudness
    return jnp.minimum(jnp.maximum(drawn, -reach), reach).astype(kind)


def setup_inputs(seed: int = 0) -> dict:
    arg_keys = jax.random.split(jax.random.key(seed), 8)
    return {
        "start_vector": bell_draw(arg_keys[0], (NSEG, NB, TILE, TILE), 1.0, 6.0, ((0, 8), (1, 32))),
        "left_environment": bell_draw(arg_keys[1], (NSEG, NB, MW, TILE, TILE), TILE ** -0.5, 0.5, ((0, 8), (1, 32))),
        "right_environment": bell_draw(arg_keys[2], (NSEG, NB, MW, TILE, TILE), TILE ** -0.5, 0.5, ((0, 8), (1, 32))),
        "block_energy": jnp.clip(jax.random.uniform(arg_keys[3], (NSEG, NB), jnp.float32, -2.0, 2.0) * block_levels(arg_keys[3], (NSEG, NB), ((0, 8), (1, 32)), -0.4, 0.0), -2.0, 2.0),
        "sector_rows": draw_sector_rows(jax.random.fold_in(arg_keys[7], 71), 0),
        "sector_cols": draw_sector_cols(jax.random.fold_in(arg_keys[7], 71), 0),
        "feed_block": draw_feed_block(jax.random.fold_in(arg_keys[7], 71), 0),
    }


epsilon = 1e-06

def live_mask(rows_live, cols_live):
    positions = jnp.arange(TILE, dtype=jnp.int32)
    row_mask = (positions[None, :] < rows_live[:, None]).astype(jnp.float32)
    col_mask = (positions[None, :] < cols_live[:, None]).astype(jnp.float32)
    return row_mask[:, :, None] * col_mask[:, None, :]

def apply_operator(vector, left_tiles, right_tiles, energy, feeds, mask_tiles):
    low_vector = lax.optimization_barrier(vector.astype(jnp.bfloat16)).astype(jnp.float32)
    half_product = jnp.einsum('kwab,kbc->kwac', left_tiles.astype(jnp.float32), low_vector)
    half_product = lax.optimization_barrier(half_product.astype(jnp.bfloat16)).astype(jnp.float32)
    contrib = jnp.einsum('kwac,kwcd->kwad', half_product, right_tiles.astype(jnp.float32))
    contrib = contrib.reshape(N_BLK, NB_DEV * MW, TILE * TILE)
    selector = (feeds.reshape(1, NB * MW) == jnp.arange(NB, dtype=jnp.int32)[:, None]).astype(jnp.float32)
    selector = selector.reshape(NB, N_BLK, NB_DEV * MW)
    partial_value = jnp.einsum('tgp,gpe->gte', selector, contrib, precision=lax.Precision.HIGHEST)
    partial_value = lax.optimization_barrier(partial_value.astype(jnp.bfloat16)).astype(jnp.float32)
    summed = lax.optimization_barrier(jnp.sum(partial_value, axis=0)).reshape(NB, TILE, TILE)
    return mask_tiles * summed + energy[:, None, None] * vector

def lanczos(start_tiles, left_tiles, right_tiles, energy, rows_live, cols_live, feeds):
    mask_tiles = live_mask(rows_live, cols_live)
    entries = float(NB * TILE * TILE)
    vector = mask_tiles * start_tiles.astype(jnp.float32)
    vector = vector * lax.rsqrt(jnp.sum(vector * vector) / entries + epsilon)
    before = jnp.zeros_like(vector)
    coef_beta = jnp.float32(0.0)
    alphas = []
    betas = []
    image = vector
    for turn_index in range(STEPS):
        image = apply_operator(vector, left_tiles, right_tiles, energy, feeds, mask_tiles)
        coef_alpha = jnp.sum(vector * image) / entries
        image = image - coef_alpha * vector - coef_beta * before
        mean_square = jnp.sum(image * image) / entries
        coef_beta = jnp.sqrt(mean_square)
        before = vector
        vector = image * lax.rsqrt(mean_square + epsilon)
        alphas.append(coef_alpha)
        betas.append(coef_beta)
    return (jnp.stack(alphas + betas).astype(jnp.float32), image)

def reference(start_vector, left_environment, right_environment, block_energy, sector_rows, sector_cols, feed_block):

    def pick_segment(array, segment):
        return lax.dynamic_index_in_dim(array, segment, 0, keepdims=False)

    def one_segment(segment):
        earlier = jnp.maximum(segment - 1, 0).astype(jnp.int32)
        left_tiles = pick_segment(left_environment, earlier)
        left_tiles = jnp.where(segment > 0, left_tiles, jnp.zeros_like(left_tiles))
        return lanczos(pick_segment(start_vector, segment), left_tiles, pick_segment(right_environment, segment), pick_segment(block_energy, segment), pick_segment(sector_rows, segment), pick_segment(sector_cols, segment), pick_segment(feed_block, segment))
    coefficients, residual = lax.map(one_segment, jnp.arange(NSEG, dtype=jnp.int32))
    return (coefficients, residual)
```

```python
import functools

import jax
import jax.numpy as jnp
from jax import lax
from jax.experimental import pallas as pl
from jax.experimental.pallas import tpu as pltpu
from jax.sharding import PartitionSpec as P

STEPS = 3
EPS = 1e-06
T = 128
NK = 4
NW = 34
NS = NK * NW
NZ, NY = 8, 4
NBLK = NZ * NY
NSEG = 8
NT = NK * NBLK
PR = 32
NP = T // PR
ENTRIES = float(NT * T * T)
F32 = jnp.float32
BF16 = jnp.bfloat16
MESH = pl.DeviceIdType.MESH


def kernel(
    start_ref,
    left_ref,
    right_ref,
    energy_ref,
    rows_ref,
    cols_ref,
    order_ref,
    goal_ref,
    last_ref,
    has_ref,
    coef_ref,
    out_ref,
    lt,
    rt,
    half,
    run,
    qa,
    qb,
    sa,
    sb,
    ra,
    rb,
    rsa,
    rsb,
    cur,
    prev,
    img,
    low,
    coef,
    mine,
    xy,
    xz,
    lt_send,
    lt_recv,
    rt_sem,
    a1_send,
    a1_recv,
    a2_send,
    a2_recv,
    b1_send,
    b1_recv,
    b2_send,
    b2_recv,
    xy_send,
    xy_recv,
    xz_send,
    xz_recv,
):
    seg = lax.axis_index("seg")
    blk = lax.axis_index("blk")
    z = blk // NY
    y = blk % NY

    def at(dz=0, dy=0, ds=0):
        zz = lax.rem(z + dz + NZ, NZ)
        yy = lax.rem(y + dy + NY, NY)
        return (lax.rem(seg + ds + NSEG, NSEG), zz * NY + yy)

    barrier = pltpu.get_barrier_semaphore()
    peers = [at(dz=d) for d in range(1, NZ)] + [at(dy=d) for d in range(1, NY)]
    peers += [at(ds=1), at(ds=-1)]
    for peer in peers:
        pl.semaphore_signal(barrier, inc=1, device_id=peer, device_id_type=MESH)
    rt_copy = pltpu.make_async_copy(right_ref, rt, rt_sem)
    rt_copy.start()
    pl.semaphore_wait(barrier, len(peers))

    def lt_copy(j, k):
        return pltpu.make_async_remote_copy(
            src_ref=left_ref.at[k, :, pl.ds(j * PR, PR), :],
            dst_ref=lt.at[j, pl.ds(k * NW, NW)],
            send_sem=lt_send.at[j, k],
            recv_sem=lt_recv.at[j, k],
            device_id=at(ds=1),
            device_id_type=MESH,
        )

    for j in range(NP):
        for k in range(NK):
            lt_copy(j, k).start()

    def total(x):
        x = jnp.sum(x.reshape(NK * T, T), axis=0, keepdims=True)
        return jnp.broadcast_to(jnp.sum(x, axis=1, keepdims=True), (1, T))

    def merged(parts):
        dots = [p[0:1] for p in parts]
        sizes = [p[1:2] for p in parts]
        means = [p[2:3] for p in parts]
        rests = [p[3:4] for p in parts]
        dot, size, rest = sum(dots[1:], dots[0]), sum(sizes[1:], sizes[0]), sum(rests[1:], rests[0])
        weighted = [m * s for m, s in zip(means, sizes)]
        weighted = sum(weighted[1:], weighted[0])
        mean = jnp.where(size > 0.0, weighted / jnp.where(size > 0.0, size, 1.0), 0.0)
        spread = [s * (m - mean) * (m - mean) for m, s in zip(means, sizes)]
        return dot, size, mean, rest + sum(spread[1:], spread[0])

    def put(n, stage, own, values):
        for i, value in enumerate(values):
            mine[n, stage, pl.ds(i, 1), :] = value
        return mine[n, stage]

    def gathered(n, stage, size, me, box, sends, recvs, move):
        copies = []
        for d in range(1, size):
            copy = pltpu.make_async_remote_copy(
                src_ref=mine.at[n, stage],
                dst_ref=box.at[n, me],
                send_sem=sends.at[n, d],
                recv_sem=recvs.at[n, d],
                device_id=move(d),
                device_id_type=MESH,
            )
            copy.start()
            copies.append(copy)
        box[n, me] = mine[n, stage]
        for copy in copies:
            copy.wait()
        return merged([box[n, i] for i in range(size)])

    def exchange(n, values):
        put(n, 0, y, values)
        values = gathered(n, 0, NY, y, xy, xy_send, xy_recv, lambda d: at(dy=d))
        put(n, 1, z, values)
        return gathered(n, 1, NZ, z, xz, xz_send, xz_recv, lambda d: at(dz=d))

    row_at = lax.broadcasted_iota(jnp.int32, (T, T), 0)
    col_at = lax.broadcasted_iota(jnp.int32, (T, T), 1)

    def mask(tile, first, rows):
        live = (row_at[:rows] + first < rows_ref[tile]) & (col_at[:rows] < cols_ref[tile])
        return live

    for i in range(NK):
        cur[i] = jnp.where(mask(i, 0, T), start_ref[i].astype(F32), 0.0)
    zero = jnp.zeros((1, T), F32)
    _, size, _, _ = exchange(STEPS, (zero, total(cur[...] * cur[...]), zero, zero))
    scale = lax.rsqrt(size / ENTRIES + EPS)
    feeds_left = (seg > 0).astype(F32)
    for i in range(NK):
        q = cur[i] * scale
        cur[i] = q
        prev[i] = jnp.zeros((T, T), F32)
        low[i] = (q * feeds_left).astype(BF16)
    coef[...] = jnp.zeros((1, T), F32)

    def ring(buf, box, sends, recvs, n, me, move):
        far = n // 2

        def parts(up, d):
            if d < far:
                return pl.ds(0, 2)
            return pl.ds(0 if up else 1, 1)

        def copy(j, up, d):
            sign = 1 if up else -1
            goal = lax.rem(me + sign * d + n, n)
            return pltpu.make_async_remote_copy(
                src_ref=buf.at[j, goal, parts(up, d)],
                dst_ref=box.at[j, 0 if up else 1, d - 1, parts(up, d)],
                send_sem=sends.at[j, 0 if up else 1, d - 1],
                recv_sem=recvs.at[j, 0 if up else 1, d - 1],
                device_id=move(sign),
                device_id_type=MESH,
            )

        def step(j, hop):
            d = far - hop
            for up in (True, False):
                if hop > 0:
                    copy(j, up, d + 1).wait_recv()
                    goal = lax.rem(me + (d if up else -d) + n, n)
                    piece = parts(up, d + 1)
                    got = box[j, 0 if up else 1, d, piece].astype(F32)
                    buf[j, goal, piece] = (buf[j, goal, piece].astype(F32) + got).astype(BF16)
                copy(j, up, d).start()

        def last(j):
            copy(j, True, 1).wait_recv()
            copy(j, False, 1).wait_recv()

        def drain(j):
            for d in range(1, far + 1):
                copy(j, True, d).wait_send()
                copy(j, False, d).wait_send()

        return step, last, drain

    up_z = lambda s: at(dz=s)
    up_y = lambda s: at(dy=s)
    a1_step, a1_last, a1_drain = ring(qa, ra, a1_send, a1_recv, NZ, z, up_z)
    a2_step, a2_last, a2_drain = ring(sa, rsa, a2_send, a2_recv, NY, y, up_y)
    b1_step, b1_last, b1_drain = ring(qb, rb, b1_send, b1_recv, NY, y, up_y)
    b2_step, b2_last, b2_drain = ring(sb, rsb, b2_send, b2_recv, NZ, z, up_z)

    def a1_final(j):
        a1_last(j)
        for h in range(2):
            for i in range(NY):
                value = qa[j, z, h, i].astype(F32) + ra[j, 0, 0, h, i].astype(F32)
                sa[j, i, h] = (value + ra[j, 1, 0, h, i].astype(F32)).astype(BF16)

    def b1_final(j):
        b1_last(j)
        for h in range(2):
            for i in range(NZ):
                value = qb[j, y, h, i].astype(F32) + rb[j, 0, 0, h, i].astype(F32)
                sb[j, i, h] = (value + rb[j, 1, 0, h, i].astype(F32)).astype(BF16)

    def image(j, tile, value):
        rows = pl.ds(j * PR, PR)
        value = jnp.where(mask(tile, j * PR, PR), value, 0.0)
        img[tile, rows] = value + energy_ref[tile] * cur[tile, rows]

    def a2_final(j):
        a2_last(j)
        for h in range(2):
            value = sa[j, y, h].astype(F32) + rsa[j, 0, 0, h].astype(F32)
            image(j, h, value + rsa[j, 1, 0, h].astype(F32))

    def b2_final(j):
        b2_last(j)
        for h in range(2):
            value = sb[j, z, h].astype(F32) + rsb[j, 0, 0, h].astype(F32)
            image(j, 2 + h, value + rsb[j, 1, 0, h].astype(F32))

    def a_life(j):
        events = [functools.partial(a1_step, j, hop) for hop in range(NZ // 2)]

        def turn():
            a1_final(j)
            a2_step(j, 0)

        events.append(turn)
        events.append(functools.partial(a2_step, j, 1))
        events.append(functools.partial(a2_final, j))
        return events

    def b_life(j):
        events = [functools.partial(b1_step, j, hop) for hop in range(NY // 2)]

        def turn():
            b1_final(j)
            b2_step(j, 0)

        events.append(turn)
        events += [functools.partial(b2_step, j, hop) for hop in range(1, NZ // 2)]
        events.append(functools.partial(b2_final, j))
        return events

    LIFE = NZ // 2 + NY // 2 + 1

    def drain():
        for j in range(NP):
            a1_drain(j)
            a2_drain(j)
            b1_drain(j)
            b2_drain(j)

    CH = 17

    def contributions(first, count):
        rows = count * PR

        def left_body(i, carry):
            for c in range(count):
                for s in range(2):
                    slot = pl.multiple_of(i * CH, CH) + s * (2 * NW)
                    k = lax.div(i * CH, NW) + 2 * s
                    tiles = lt[first + c, pl.ds(slot, CH)].reshape(CH * PR, T)
                    value = jnp.dot(tiles, low[k], preferred_element_type=F32).astype(BF16)
                    half[pl.ds(slot, CH), pl.ds(c * PR, PR)] = value.reshape(CH, PR, T)
            return carry

        lax.fori_loop(0, NS // (2 * CH), left_body, 0)

        UN = 8

        def right_body(i, acc):
            values = []
            for n in range(UN):
                slot = order_ref[i * UN + n]
                values.append(
                    jnp.dot(half[slot, pl.ds(0, rows)], rt[slot], preferred_element_type=F32)
                )
            for n in range(UN):
                here = i * UN + n
                before = jnp.maximum(here - 1, 0)
                same = goal_ref[here] == goal_ref[before]
                acc = jnp.where(same, acc, 0.0) + values[n]
                run[here, pl.ds(0, rows)] = acc.astype(BF16)
            return acc

        lax.fori_loop(0, NS // UN, right_body, jnp.zeros((rows, T), F32))

        def pick(o, carry):
            zo, yo = lax.div(o, NY), lax.rem(o, NY)
            for tile in range(NK):
                t = o * NK + tile
                value = run[last_ref[t], pl.ds(0, rows)]
                value = jnp.where(has_ref[t] > 0, value, jnp.zeros_like(value))
                for c in range(count):
                    part = value[c * PR : (c + 1) * PR]
                    if tile < 2:
                        qa[first + c, zo, tile, yo] = part
                    else:
                        qb[first + c, yo, tile - 2, zo] = part
            return carry

        lax.fori_loop(0, NBLK, pick, 0)

    def finish(n, beta, last):
        q, u = cur[...], img[...]
        g = u - beta * prev[...]
        dot = total(q * u)
        size = total(q * q)
        along = total(q * g)
        mean = jnp.where(size > 0.0, along / jnp.where(size > 0.0, size, 1.0), 0.0)
        rest = g - mean * q
        rest = total(rest * rest)
        dot, size, mean, rest = exchange(n, (dot, size, mean, rest))
        alpha = dot / ENTRIES
        square = (rest + size * (mean - alpha) * (mean - alpha)) / ENTRIES
        new_beta = jnp.sqrt(square)
        scale = lax.rsqrt(square + EPS)
        lane = lax.broadcasted_iota(jnp.int32, (1, T), 1)
        value = jnp.where(lane == n, alpha, coef[...])
        coef[...] = jnp.where(lane == n + STEPS, new_beta, value)
        for i in range(NK):
            q = cur[i]
            u = img[i] - alpha * q - beta * prev[i]
            if last:
                out_ref[i] = u
            else:
                prev[i] = q
                u = u * scale
                cur[i] = u
                low[i] = (u * feeds_left).astype(BF16)
        return new_beta

    lives = [(a_life(j), b_life(j)) for j in range(NP)]

    def play(j, n):
        if 0 <= n < LIFE:
            for life in lives[j]:
                life[n]()

    rt_copy.wait()
    for turn in range(NP + LIFE - 1):
        if turn < NP:
            for k in range(NK):
                lt_copy(turn, k).wait_recv()
            contributions(turn, 1)
        for j in range(NP):
            play(j, turn - j)
    drain()
    for j in range(NP):
        for k in range(NK):
            lt_copy(j, k).wait_send()
    beta = finish(0, zero, False)

    for n in range(1, STEPS):
        contributions(0, 2)
        for j in (0, 1):
            play(j, 0)
        contributions(2, 2)
        for turn in range(1, LIFE + 1):
            for j in (0, 1):
                play(j, turn)
            for j in (2, 3):
                play(j, turn - 1)
        drain()
        beta = finish(n, beta, n == STEPS - 1)
    coef_ref[...] = coef[:, : 2 * STEPS]


def local(start, left, right, energy, rows, cols, feeds):
    feeds = feeds.reshape(NS)
    slots = jnp.arange(NS, dtype=jnp.int32)
    ahead = (feeds[None, :] < feeds[:, None]) | (
        (feeds[None, :] == feeds[:, None]) & (slots[None, :] < slots[:, None])
    )
    rank = jnp.sum(ahead.astype(jnp.int32), axis=1)
    here = rank[:, None] == slots[None, :]
    order = jnp.sum(jnp.where(here, slots[:, None], 0), axis=0)
    goal = jnp.sum(jnp.where(here, feeds[:, None], 0), axis=0)
    targets = jnp.arange(NT, dtype=jnp.int32)
    upto = jnp.sum((feeds[:, None] <= targets[None, :]).astype(jnp.int32), axis=0)
    has = jnp.sum((feeds[:, None] == targets[None, :]).astype(jnp.int32), axis=0)
    last = jnp.maximum(upto - 1, 0)

    vmem = pl.BlockSpec(memory_space=pltpu.VMEM)
    smem = pl.BlockSpec(memory_space=pltpu.SMEM)
    hbm = pl.BlockSpec(memory_space=pl.ANY)
    dma = pltpu.SemaphoreType.DMA
    coef, residual = pl.pallas_call(
        kernel,
        out_shape=(
            jax.ShapeDtypeStruct((1, 2 * STEPS), F32),
            jax.ShapeDtypeStruct((NK, T, T), F32),
        ),
        in_specs=[vmem, hbm, hbm] + [smem] * 7,
        out_specs=(vmem, vmem),
        scratch_shapes=[
            pltpu.VMEM((NP, NS, PR, T), BF16),
            pltpu.VMEM((NS, T, T), BF16),
            pltpu.VMEM((NS, 2 * PR, T), BF16),
            pltpu.VMEM((NS, 2 * PR, T), BF16),
            pltpu.VMEM((NP, NZ, 2, NY, PR, T), BF16),
            pltpu.VMEM((NP, NY, 2, NZ, PR, T), BF16),
            pltpu.VMEM((NP, NY, 2, PR, T), BF16),
            pltpu.VMEM((NP, NZ, 2, PR, T), BF16),
            pltpu.VMEM((NP, 2, NZ // 2, 2, NY, PR, T), BF16),
            pltpu.VMEM((NP, 2, NY // 2, 2, NZ, PR, T), BF16),
            pltpu.VMEM((NP, 2, NY // 2, 2, PR, T), BF16),
            pltpu.VMEM((NP, 2, NZ // 2, 2, PR, T), BF16),
            pltpu.VMEM((NK, T, T), F32),
            pltpu.VMEM((NK, T, T), F32),
            pltpu.VMEM((NK, T, T), F32),
            pltpu.VMEM((NK, T, T), BF16),
            pltpu.VMEM((1, T), F32),
            pltpu.VMEM((STEPS + 1, 2, 8, T), F32),
            pltpu.VMEM((STEPS + 1, NY, 8, T), F32),
            pltpu.VMEM((STEPS + 1, NZ, 8, T), F32),
            dma((NP, NK)),
            dma((NP, NK)),
            dma,
            dma((NP, 2, NZ // 2)),
            dma((NP, 2, NZ // 2)),
            dma((NP, 2, NY // 2)),
            dma((NP, 2, NY // 2)),
            dma((NP, 2, NY // 2)),
            dma((NP, 2, NY // 2)),
            dma((NP, 2, NZ // 2)),
            dma((NP, 2, NZ // 2)),
            dma((STEPS + 1, NY)),
            dma((STEPS + 1, NY)),
            dma((STEPS + 1, NZ)),
            dma((STEPS + 1, NZ)),
        ],
        compiler_params=pltpu.CompilerParams(
            collective_id=0, has_side_effects=True, vmem_limit_bytes=48 * 2**20
        ),
        cost_estimate=pl.CostEstimate(
            flops=STEPS * NS * 4 * T**3, bytes_accessed=4 * NS * T * T, transcendentals=0
        ),
        name="lanczos",
    )(
        start[0],
        left[0],
        right[0].reshape(NS, T, T),
        energy[0],
        rows[0],
        cols[0],
        order,
        goal,
        last,
        has,
    )
    return coef, residual[None]


def solution(mesh):
    return jax.shard_map(
        local,
        mesh=mesh,
        in_specs=(
            P("seg", "blk", None, None),
            P("seg", "blk", None, None, None),
            P("seg", "blk", None, None, None),
            P("seg", "blk"),
            P("seg", "blk"),
            P("seg", "blk"),
            P("seg", "blk", None),
        ),
        out_specs=(P("seg", None), P("seg", "blk", None, None)),
        check_vma=False,
    )
```

```python
import functools

import jax
import jax.numpy as jnp
from jax import lax
from jax.experimental import pallas as pl
from jax.experimental.pallas import tpu as pltpu
from jax.sharding import PartitionSpec as P

STEPS = 3
EPS = 1e-06
T = 128
NK = 4
NW = 34
NS = NK * NW
NZ, NY = 8, 4
NBLK = NZ * NY
NSEG = 8
NT = NK * NBLK
PR = 32
NP = T // PR
HR = PR // 2
NA = (2, 2, 1, 1)
A2_DIRECT = (True,) * NP
B2_ROUNDS = (2, 2, 2, 2)
ENTRIES = float(NT * T * T)
F32 = jnp.float32
BF16 = jnp.bfloat16
MESH = pl.DeviceIdType.MESH


def kernel(
    start_hbm,
    left_ref,
    right_ref,
    energy_hbm,
    rows_hbm,
    cols_hbm,
    order_hbm,
    goal_hbm,
    last_hbm,
    has_hbm,
    coef_ref,
    out_ref,
    start_ref,
    scalars,
    scalar_sem,
    lt,
    rt,
    half,
    run,
    qa,
    qb,
    sa,
    sb,
    ra,
    rb,
    rsa,
    rsb,
    cur,
    prev,
    img,
    near,
    ahead,
    low,
    coef,
    mine,
    xy,
    xz,
    lt_send,
    lt_recv,
    rt_sem,
    a1_send,
    a1_recv,
    a2_send,
    a2_recv,
    b1_send,
    b1_recv,
    b2_send,
    b2_recv,
    xy_send,
    xy_recv,
    xz_send,
    xz_recv,
):
    seg = lax.axis_index("seg")
    blk = lax.axis_index("blk")
    z = blk // NY
    y = blk % NY

    def at(dz=0, dy=0, ds=0):
        zz = lax.rem(z + dz + NZ, NZ)
        yy = lax.rem(y + dy + NY, NY)
        return (lax.rem(seg + ds + NSEG, NSEG), zz * NY + yy)

    barrier = pltpu.get_barrier_semaphore()
    peers = [at(ds=1), at(ds=-1)]
    peers += [at(dz=d) for d in (4, 3, 5, 2, 6, 1, 7)] + [at(dy=d) for d in (2, 1, 3)]
    for peer in peers:
        pl.semaphore_signal(barrier, inc=1, device_id=peer, device_id_type=MESH)
    energy_ref, rows_ref, cols_ref, order_ref, goal_ref, last_ref, has_ref = scalars
    local_copies = [pltpu.make_async_copy(start_hbm, start_ref, scalar_sem.at[7])]
    sources = (energy_hbm, rows_hbm, cols_hbm, order_hbm, goal_hbm, last_hbm, has_hbm)
    for i, (source, goal) in enumerate(zip(sources, scalars)):
        local_copies.append(pltpu.make_async_copy(source, goal, scalar_sem.at[i]))
    local_copies.append(pltpu.make_async_copy(right_ref, rt, rt_sem))
    for copy in local_copies:
        copy.start()
    pl.semaphore_wait(barrier, len(peers))

    def lt_copy(j, k):
        return pltpu.make_async_remote_copy(
            src_ref=left_ref.at[k, :, pl.ds(j * PR, PR), :],
            dst_ref=lt.at[j, pl.ds(k * NW, NW)],
            send_sem=lt_send.at[j, k],
            recv_sem=lt_recv.at[j, k],
            device_id=at(ds=1),
            device_id_type=MESH,
        )

    for j in range(NP):
        for k in range(NK):
            lt_copy(j, k).start()
    for copy in local_copies:
        copy.wait()

    def total(parts):
        x = sum(parts[1:], parts[0])
        x = jnp.sum(x, axis=0, keepdims=True)
        return jnp.broadcast_to(jnp.sum(x, axis=1, keepdims=True), (1, T))

    def merged(parts):
        rows = [[p[i : i + 1] for p in parts] for i in range(7)]
        add = lambda values: sum(values[1:], values[0])
        sizes, means = rows[1], rows[2]
        size = add(sizes)
        weighted = add([m * s for m, s in zip(means, sizes)])
        mean = jnp.where(size > 0.0, weighted / jnp.where(size > 0.0, size, 1.0), 0.0)
        spread = add([s * (m - mean) * (m - mean) for m, s in zip(means, sizes)])
        return [add(rows[0]), size, mean, add(rows[3]) + spread] + [add(r) for r in rows[4:]]

    def copies_of(n, stage, size, me, box, sends, recvs, move, order):
        return [
            pltpu.make_async_remote_copy(
                src_ref=mine.at[n, stage],
                dst_ref=box.at[n, me],
                send_sem=sends.at[n, d],
                recv_sem=recvs.at[n, d],
                device_id=move(d),
                device_id_type=MESH,
            )
            for d in order
        ]

    def stage_y(n):
        return copies_of(n, 0, NY, y, xy, xy_send, xy_recv, lambda d: at(dy=d), (2, 1, 3))

    def stage_z(n):
        order = (4, 3, 5, 2, 6, 1, 7)
        return copies_of(n, 1, NZ, z, xz, xz_send, xz_recv, lambda d: at(dz=d), order)

    def post(n, stage, values, copies, box, me):
        for i, value in enumerate(values):
            mine[n, stage, pl.ds(i, 1), :] = value
        for copy in copies:
            copy.start()
        box[n, me] = mine[n, stage]

    def exchange_open(n, values):
        post(n, 0, values, stage_y(n), xy, y)

    def exchange_pass(n):
        for copy in stage_y(n):
            copy.wait()
        post(n, 1, merged([xy[n, i] for i in range(NY)]), stage_z(n), xz, z)

    def exchange_close(n):
        for copy in stage_z(n):
            copy.wait()
        return merged([xz[n, i] for i in range(NZ)])

    row_at = lax.broadcasted_iota(jnp.int32, (T, T), 0)
    col_at = lax.broadcasted_iota(jnp.int32, (T, T), 1)

    def mask(tile, first, rows):
        return (row_at[:rows] + first < rows_ref[tile]) & (col_at[:rows] < cols_ref[tile])

    def mean_energy(weighted, size):
        value = jnp.where(size > 0.0, weighted / jnp.where(size > 0.0, size, 1.0), 0.0)
        return jnp.clip(value, -2.0, 2.0)

    zero = jnp.zeros((1, T), F32)
    squares = []
    for i in range(NK):
        q = jnp.where(mask(i, 0, T), start_ref[i].astype(F32), 0.0)
        cur[i] = q
        squares.append(q * q)
    weighted = total([square * energy_ref[i] for i, square in enumerate(squares)])
    exchange_open(STEPS, [zero, total(squares), zero, zero, weighted, zero, zero])
    exchange_pass(STEPS)
    _, size, _, _, weighted, _, _ = exchange_close(STEPS)
    scale = lax.rsqrt(size / ENTRIES + EPS)
    shift = mean_energy(weighted, size)
    feeds_left = (seg > 0).astype(F32)
    for i in range(NK):
        q = cur[i] * scale
        cur[i] = q
        prev[i] = jnp.zeros((T, T), F32)
        near[i] = jnp.zeros((T, T), F32)
        low[i] = (q * feeds_left).astype(BF16)
    coef[...] = jnp.zeros((1, T), F32)

    def ring(side, bufs, boxes, sends, recvs, n, me, move):
        far = n // 2

        def parts(up, d):
            if d < far:
                return pl.ds(0, 2)
            return pl.ds(0 if up else 1, 1)

        def copy(j, up, d):
            sign = 1 if up else -1
            goal = lax.rem(me + sign * d + n, n)
            return pltpu.make_async_remote_copy(
                src_ref=bufs[j].at[goal, parts(up, d)],
                dst_ref=boxes[j].at[side, 0 if up else 1, d - 1, parts(up, d)],
                send_sem=sends.at[side * NP + j, 0 if up else 1, d - 1],
                recv_sem=recvs.at[side * NP + j, 0 if up else 1, d - 1],
                device_id=move(sign),
                device_id_type=MESH,
            )

        def step(j, hop):
            d = far - hop
            for up in (True, False):
                if hop > 0:
                    copy(j, up, d + 1).wait_recv()
                    goal = lax.rem(me + (d if up else -d) + n, n)
                    piece = parts(up, d + 1)
                    got = boxes[j][side, 0 if up else 1, d, piece].astype(F32)
                    own = bufs[j][goal, piece].astype(F32)
                    bufs[j][goal, piece] = (own + got).astype(BF16)
                copy(j, up, d).start()

        def last(j, h):
            return [boxes[j][side, i, 0, h] for i in range(2)]

        def arrive(j):
            copy(j, True, 1).wait_recv()
            copy(j, False, 1).wait_recv()

        def drain(j):
            for d in range(1, far + 1):
                copy(j, True, d).wait_send()
                copy(j, False, d).wait_send()

        return step, arrive, last, drain

    def direct(side, bufs, boxes, sends, recvs, n, me, move):
        far = n // 2
        order = sorted(range(1, n), key=lambda d: -min(d, n - d))

        def copy(j, d):
            at_box = ((d - 1) // far, (d - 1) % far)
            return pltpu.make_async_remote_copy(
                src_ref=bufs[j].at[lax.rem(me + d, n)],
                dst_ref=boxes[j].at[(side,) + at_box],
                send_sem=sends.at[(side * NP + j,) + at_box],
                recv_sem=recvs.at[(side * NP + j,) + at_box],
                device_id=move(d),
                device_id_type=MESH,
            )

        def step(j, hop):
            for d in order:
                copy(j, d).start()

        def arrive(j):
            for d in order:
                copy(j, d).wait_recv()

        def last(j, h):
            return [boxes[j][side, (d - 1) // far, (d - 1) % far, h] for d in range(1, n)]

        def drain(j):
            for d in order:
                copy(j, d).wait_send()

        return step, arrive, last, drain

    def relay(side, bufs, boxes, sends, recvs, n, me, move):
        far = n // 2
        rounds = [(up, d) for d in range(far, 0, -1) for up in (True, False)]

        def parts(up, d):
            if d < far:
                return pl.ds(0, 2)
            return pl.ds(0 if up else 1, 1)

        def copy(j, up, d):
            sign = 1 if up else -1
            row = 0 if up else 1
            return pltpu.make_async_remote_copy(
                src_ref=bufs[j].at[lax.rem(me + sign * d + n, n), parts(up, d)],
                dst_ref=boxes[j].at[side, row, d - 1, parts(up, d)],
                send_sem=sends.at[side * NP + j, row, d - 1],
                recv_sem=recvs.at[side * NP + j, row, d - 1],
                device_id=move(sign * max(d - 1, 1)),
                device_id_type=MESH,
            )

        def step(j, hop):
            if hop == 0:
                for up, d in rounds[:-2]:
                    copy(j, up, d).start()
                return
            for up, d in rounds[:-2]:
                copy(j, up, d).wait_recv()
            for up in (True, False):
                row = 0 if up else 1
                goal = lax.rem(me + (1 if up else -1) + n, n)
                for h in range(2):
                    reach = range(2, far + 1 if h == row else far)
                    terms = [boxes[j][side, row, d - 1, h] for d in reach]
                    bufs[j][goal, h] = add([bufs[j][goal, h]] + terms).astype(BF16)
                copy(j, up, 1).start()

        def arrive(j):
            copy(j, True, 1).wait_recv()
            copy(j, False, 1).wait_recv()

        def last(j, h):
            return [boxes[j][side, i, 0, h] for i in range(2)]

        def drain(j):
            for up, d in rounds:
                copy(j, up, d).wait_send()

        return step, arrive, last, drain

    up_z = lambda s: at(dz=s)
    up_y = lambda s: at(dy=s)
    def add(values):
        values = [value.astype(F32) for value in values]
        return sum(values[1:], values[0])

    def turn_over(j, stage, src, me, goals, count, wide):
        _, arrive, last, _ = stage
        arrive(j)
        for h in range(2):
            got = last(j, h)
            for c in range(count):
                for i in range(wide):
                    value = add([src[j][me, h, c, i]] + [g[c, i] for g in got])
                    goals[j][i, h, c] = value.astype(BF16)

    def image(j, tile, h, value):
        first = j * PR + h * HR
        img[tile, pl.ds(first, HR)] = jnp.where(mask(tile, first, HR), value, 0.0)

    def into_image(j, stage, src, me, count, first_tile):
        _, arrive, last, _ = stage
        arrive(j)
        for h in range(2):
            got = last(j, h)
            for c in range(count):
                image(j, first_tile + c, h, add([src[j][me, h, c]] + [g[c] for g in got]))

    def network(side):
        a1 = ring(side, qa, ra, a1_send, a1_recv, NZ, z, up_z)
        b1 = ring(side, qb, rb, b1_send, b1_recv, NY, y, up_y)
        a2_args = (side, sa, rsa, a2_send, a2_recv, NY, y, up_y)
        b2_args = (side, sb, rsb, b2_send, b2_recv, NZ, z, up_z)
        a2_of = [(direct if flag else ring)(*a2_args) for flag in A2_DIRECT]
        b2_of = [{1: direct, 2: relay, 4: ring}[r](*b2_args) for r in B2_ROUNDS]

        def a_life(j):
            events = [functools.partial(a1[0], j, hop) for hop in range(NZ // 2)]

            def turn():
                turn_over(j, a1, qa, z, sa, NA[j], NY)
                a2_of[j][0](j, 0)

            events.append(turn)
            if not A2_DIRECT[j]:
                events += [functools.partial(a2_of[j][0], j, hop) for hop in range(1, NY // 2)]
            events.append(lambda: into_image(j, a2_of[j], sa, y, NA[j], 0))
            return events

        def b_life(j):
            events = [functools.partial(b1[0], j, hop) for hop in range(NY // 2)]

            def turn():
                turn_over(j, b1, qb, y, sb, NK - NA[j], NZ)
                b2_of[j][0](j, 0)

            events.append(turn)
            events += [functools.partial(b2_of[j][0], j, hop) for hop in range(1, B2_ROUNDS[j])]
            events.append(lambda: into_image(j, b2_of[j], sb, z, NK - NA[j], NA[j]))
            return events

        lives = [(a_life(j), b_life(j)) for j in range(NP)]
        life_of = [max(len(a), len(b)) for a, b in lives]

        def play(j, n):
            for life in lives[j]:
                if 0 <= n < len(life):
                    life[n]()

        def drain():
            for j in range(NP):
                for stage in (a1, b1, a2_of[j], b2_of[j]):
                    stage[3](j)

        return play, drain, max(life_of)

    networks = [network(0), network(1)]

    CH = 17
    UN = 8

    def contributions(first, count):
        rows = count * PR

        def left_body(i, carry):
            for c in range(count):
                for s in range(2):
                    slot = pl.multiple_of(i * CH, CH) + s * (2 * NW)
                    k = lax.div(i * CH, NW) + 2 * s
                    tiles = lt[first + c, pl.ds(slot, CH)].reshape(CH * PR, T)
                    value = jnp.dot(tiles, low[k], preferred_element_type=F32).astype(BF16)
                    half[pl.ds(slot, CH), pl.ds(c * PR, PR)] = value.reshape(CH, PR, T)
            return carry

        lax.fori_loop(0, NS // (2 * CH), left_body, 0)

        def right_body(i, acc):
            values = []
            for n in range(UN):
                slot = order_ref[i * UN + n]
                values.append(
                    jnp.dot(half[slot, pl.ds(0, rows)], rt[slot], preferred_element_type=F32)
                )
            for n in range(UN):
                here = i * UN + n
                before = jnp.maximum(here - 1, 0)
                same = goal_ref[here] == goal_ref[before]
                acc = jnp.where(same, acc, 0.0) + values[n]
                run[here, pl.ds(0, rows)] = acc.astype(BF16)
            return acc

        lax.fori_loop(0, NS // UN, right_body, jnp.zeros((rows, T), F32))

        def pick(o, carry):
            zo, yo = lax.div(o, NY), lax.rem(o, NY)
            for tile in range(NK):
                t = o * NK + tile
                value = run[last_ref[t], pl.ds(0, rows)]
                value = jnp.where(has_ref[t] > 0, value, jnp.zeros_like(value))
                for c in range(count):
                    for h in range(2):
                        part = value[c * PR + h * HR : c * PR + (h + 1) * HR]
                        j = first + c
                        if tile < NA[j]:
                            qa[j][zo, h, tile, yo] = part
                        else:
                            qb[j][yo, h, tile - NA[j], zo] = part
            return carry

        lax.fori_loop(0, NBLK, pick, 0)

    def settle(extra, scale, beta, shift):
        for i in range(NK):
            n_q = img[i]
            if scale is not None:
                n_q = (n_q - extra * near[i]) * scale
            near[i] = n_q
            g = n_q + (energy_ref[i] - shift) * cur[i] - beta * prev[i]
            ahead[i] = g
            low[i] = (g * feeds_left).astype(BF16)

    def sums(shift):
        dots, sizes, alongs, ones, twos, threes = [], [], [], [], [], []
        for i in range(NK):
            q, w, e = cur[i], ahead[i], energy_ref[i]
            dots.append(q * (near[i] + e * q))
            sizes.append(q * q)
            alongs.append(q * w)
            ones.append(e * (w * w))
            twos.append(e * (w * q))
            threes.append(e * (q * q))
        size, along = total(sizes), total(alongs)
        mean = jnp.where(size > 0.0, along / jnp.where(size > 0.0, size, 1.0), 0.0)
        rests = []
        for i in range(NK):
            rest = ahead[i] - mean * cur[i]
            rests.append(rest * rest)
        return [
            total(dots), size, mean, total(rests), total(ones), total(twos), total(threes),
        ]

    def conclude(n, shift):
        dot, size, mean, rest, one, two, three = exchange_close(n)
        alpha = dot / ENTRIES
        extra = alpha - shift
        whole = rest + size * (mean - extra) * (mean - extra)
        square = whole / ENTRIES
        beta = jnp.sqrt(square)
        lane = lax.broadcasted_iota(jnp.int32, (1, T), 1)
        value = jnp.where(lane == n, alpha, coef[...])
        coef[...] = jnp.where(lane == n + STEPS, beta, value)
        next_shift = mean_energy(one - 2.0 * extra * two + extra * extra * three, whole)
        return extra, lax.rsqrt(square + EPS), beta, next_shift

    play, drain, turns = networks[0]
    for j in range(NP):
        for i in range(j):
            play(i, 2 * (j - i) - 1)
        for k in range(NK):
            lt_copy(j, k).wait_recv()
        contributions(j, 1)
        for i in range(j + 1):
            play(i, 2 * (j - i))
    for turn in range(1, turns):
        for j in range(NP):
            play(j, 2 * (NP - 1 - j) + turn)
    drain()
    for j in range(NP):
        for k in range(NK):
            lt_copy(j, k).wait_send()
    settle(None, None, zero, shift)

    for n in range(1, STEPS):
        play, drain, turns = networks[n % 2]
        contributions(0, NP)
        for j in range(NP):
            play(j, 0)
        exchange_open(n - 1, sums(shift))
        extra = scale = beta = None
        for turn in range(1, turns):
            for j in range(NP):
                play(j, turn)
            if turn == 1:
                exchange_pass(n - 1)
            if turn == 3:
                extra, scale, beta, next_shift = conclude(n - 1, shift)
                shift = next_shift
                for i in range(NK):
                    q = cur[i]
                    prev[i] = q
                    cur[i] = (ahead[i] - extra * q) * scale
        drain()
        settle(extra, scale, beta, shift)
    exchange_open(STEPS - 1, sums(shift))
    exchange_pass(STEPS - 1)
    extra, _, _, _ = conclude(STEPS - 1, shift)
    for i in range(NK):
        out_ref[i] = ahead[i] - extra * cur[i]
    coef_ref[...] = coef[:, : 2 * STEPS]


def local(start, left, right, energy, rows, cols, feeds):
    feeds = feeds.reshape(NS)
    slots = jnp.arange(NS, dtype=jnp.int32)
    ahead = (feeds[None, :] < feeds[:, None]) | (
        (feeds[None, :] == feeds[:, None]) & (slots[None, :] < slots[:, None])
    )
    rank = jnp.sum(ahead.astype(jnp.int32), axis=1)
    here = rank[:, None] == slots[None, :]
    order = jnp.sum(jnp.where(here, slots[:, None], 0), axis=0)
    goal = jnp.sum(jnp.where(here, feeds[:, None], 0), axis=0)
    targets = jnp.arange(NT, dtype=jnp.int32)
    upto = jnp.sum((feeds[:, None] <= targets[None, :]).astype(jnp.int32), axis=0)
    has = jnp.sum((feeds[:, None] == targets[None, :]).astype(jnp.int32), axis=0)
    last = jnp.maximum(upto - 1, 0)

    vmem = pl.BlockSpec(memory_space=pltpu.VMEM)
    hbm = pl.BlockSpec(memory_space=pl.ANY)
    dma = pltpu.SemaphoreType.DMA

    def piecewise(shape):
        return [pltpu.VMEM(shape(na, NK - na), BF16) for na in NA]

    coef, residual = pl.pallas_call(
        kernel,
        out_shape=(
            jax.ShapeDtypeStruct((1, 2 * STEPS), F32),
            jax.ShapeDtypeStruct((NK, T, T), F32),
        ),
        in_specs=[hbm] * 10,
        out_specs=(vmem, vmem),
        scratch_shapes=[
            pltpu.VMEM((NK, T, T), BF16),
            [pltpu.SMEM((NK,), F32)]
            + [pltpu.SMEM((size,), jnp.int32) for size in (NK, NK, NS, NS, NT, NT)],
            dma((8,)),
            pltpu.VMEM((NP, NS, PR, T), BF16),
            pltpu.VMEM((NS, T, T), BF16),
            pltpu.VMEM((NS, T, T), BF16),
            pltpu.VMEM((NS, T, T), BF16),
            piecewise(lambda na, nb: (NZ, 2, na, NY, HR, T)),
            piecewise(lambda na, nb: (NY, 2, nb, NZ, HR, T)),
            piecewise(lambda na, nb: (NY, 2, na, HR, T)),
            piecewise(lambda na, nb: (NZ, 2, nb, HR, T)),
            piecewise(lambda na, nb: (2, 2, NZ // 2, 2, na, NY, HR, T)),
            piecewise(lambda na, nb: (2, 2, NY // 2, 2, nb, NZ, HR, T)),
            piecewise(lambda na, nb: (2, 2, NY // 2, 2, na, HR, T)),
            piecewise(lambda na, nb: (2, 2, NZ // 2, 2, nb, HR, T)),
            pltpu.VMEM((NK, T, T), F32),
            pltpu.VMEM((NK, T, T), F32),
            pltpu.VMEM((NK, T, T), F32),
            pltpu.VMEM((NK, T, T), F32),
            pltpu.VMEM((NK, T, T), F32),
            pltpu.VMEM((NK, T, T), BF16),
            pltpu.VMEM((1, T), F32),
            pltpu.VMEM((STEPS + 1, 2, 8, T), F32),
            pltpu.VMEM((STEPS + 1, NY, 8, T), F32),
            pltpu.VMEM((STEPS + 1, NZ, 8, T), F32),
            dma((NP, NK)),
            dma((NP, NK)),
            dma,
            dma((2 * NP, 2, NZ // 2)),
            dma((2 * NP, 2, NZ // 2)),
            dma((2 * NP, 2, NY // 2)),
            dma((2 * NP, 2, NY // 2)),
            dma((2 * NP, 2, NY // 2)),
            dma((2 * NP, 2, NY // 2)),
            dma((2 * NP, 2, NZ // 2)),
            dma((2 * NP, 2, NZ // 2)),
            dma((STEPS + 1, NY)),
            dma((STEPS + 1, NY)),
            dma((STEPS + 1, NZ)),
            dma((STEPS + 1, NZ)),
        ],
        compiler_params=pltpu.CompilerParams(
            collective_id=0, has_side_effects=True, vmem_limit_bytes=60 * 2**20
        ),
        cost_estimate=pl.CostEstimate(
            flops=STEPS * NS * 4 * T**3, bytes_accessed=4 * NS * T * T, transcendentals=0
        ),
        name="lanczos",
    )(
        start[0],
        left[0],
        right[0].reshape(NS, T, T),
        energy[0],
        rows[0],
        cols[0],
        order,
        goal,
        last,
        has,
    )
    return coef, residual[None]


def solution(mesh):
    return jax.shard_map(
        local,
        mesh=mesh,
        in_specs=(
            P("seg", "blk", None, None),
            P("seg", "blk", None, None, None),
            P("seg", "blk", None, None, None),
            P("seg", "blk"),
            P("seg", "blk"),
            P("seg", "blk"),
            P("seg", "blk", None),
        ),
        out_specs=(P("seg", None), P("seg", "blk", None, None)),
        check_vma=False,
    )
```

```python
import functools

import jax
import jax.numpy as jnp
from jax import lax
from jax.experimental import pallas as pl
from jax.experimental.pallas import tpu as pltpu
from jax.sharding import PartitionSpec as P

STEPS = 3
EPS = 1e-06
T = 128
NK = 4
NW = 34
NS = NK * NW
NZ, NY = 8, 4
NBLK = NZ * NY
NSEG = 8
NT = NK * NBLK
PR = 32
NP = T // PR
HR = PR // 2
NX = 14
NA = (2, 2, 1, 1)
A2_DIRECT = (True,) * NP
B2_ROUNDS = (2, 2, 2, 2)
ENTRIES = float(NT * T * T)
F32 = jnp.float32
BF16 = jnp.bfloat16
MESH = pl.DeviceIdType.MESH


def kernel(
    start_hbm,
    left_ref,
    right_ref,
    energy_hbm,
    rows_hbm,
    cols_hbm,
    order_hbm,
    goal_hbm,
    last_hbm,
    has_hbm,
    coef_ref,
    out_ref,
    start_ref,
    scalars,
    scalar_sem,
    lt,
    rt,
    half,
    run,
    qa,
    qb,
    sa,
    sb,
    ra,
    rb,
    rsa,
    rsb,
    cur,
    prev,
    img,
    near,
    ahead,
    low,
    coef,
    mine,
    xy,
    xz,
    lt_send,
    lt_recv,
    round_box,
    round_send,
    round_recv,
    rt_sem,
    a1_send,
    a1_recv,
    a2_send,
    a2_recv,
    b1_send,
    b1_recv,
    b2_send,
    b2_recv,
    xy_send,
    xy_recv,
    xz_send,
    xz_recv,
):
    seg = lax.axis_index("seg")
    blk = lax.axis_index("blk")
    z = blk // NY
    y = blk % NY

    def at(dz=0, dy=0, ds=0):
        zz = lax.rem(z + dz + NZ, NZ)
        yy = lax.rem(y + dy + NY, NY)
        return (lax.rem(seg + ds + NSEG, NSEG), zz * NY + yy)

    barrier = pltpu.get_barrier_semaphore()
    peers = [at(ds=1), at(ds=-1)]
    peers += [at(dz=d) for d in (4, 3, 5, 2, 6, 1, 7)] + [at(dy=d) for d in (2, 1, 3)]
    for peer in peers:
        pl.semaphore_signal(barrier, inc=1, device_id=peer, device_id_type=MESH)
    odd = lax.rem(seg, 2)

    @pl.when(odd == 1)
    def _():
        for ds in (2, -2, -3):
            pl.semaphore_signal(barrier, inc=1, device_id=at(ds=ds), device_id_type=MESH)

    @pl.when(odd == 0)
    def _():
        pl.semaphore_signal(barrier, inc=1, device_id=at(ds=3), device_id_type=MESH)

    energy_ref, rows_ref, cols_ref, order_ref, goal_ref, last_ref, has_ref = scalars
    local_copies = [pltpu.make_async_copy(start_hbm, start_ref, scalar_sem.at[7])]
    sources = (energy_hbm, rows_hbm, cols_hbm, order_hbm, goal_hbm, last_hbm, has_hbm)
    for i, (source, goal) in enumerate(zip(sources, scalars)):
        local_copies.append(pltpu.make_async_copy(source, goal, scalar_sem.at[i]))
    local_copies.append(pltpu.make_async_copy(right_ref, rt, rt_sem))
    for copy in local_copies:
        copy.start()
    pl.semaphore_wait(barrier, len(peers) + 1 + 2 * odd)

    def lt_copy(j, k):
        tile = min(k, NK - 1)
        first, count = ((0, NW), (0, NW - NX), (NW - NX, NX))[max(k - NK + 2, 0)]
        return pltpu.make_async_remote_copy(
            src_ref=left_ref.at[tile, pl.ds(first, count), pl.ds(j * PR, PR), :],
            dst_ref=lt.at[j, pl.ds(tile * NW + first, count)],
            send_sem=lt_send.at[j, k],
            recv_sem=lt_recv.at[j, k],
            device_id=at(ds=1),
            device_id_type=MESH,
        )

    def round_copy(j, hop):
        source = left_ref.at[NK - 1, pl.ds(NW - NX, NX), pl.ds(j * PR, PR), :]
        return pltpu.make_async_remote_copy(
            src_ref=source if hop == 0 else round_box.at[hop - 1, j],
            dst_ref=lt.at[j, pl.ds(NS - NX, NX)] if hop == 2 else round_box.at[hop, j],
            send_sem=round_send.at[hop, j],
            recv_sem=lt_recv.at[j, NK] if hop == 2 else round_recv.at[hop, j],
            device_id=at(ds=-3) if hop == 2 else at(ds=-2),
            device_id_type=MESH,
        )

    def pass_round(*moves):
        @pl.when(odd == 1)
        def _():
            for j, hop in moves:
                round_copy(j, hop - 1).wait_recv()
                round_copy(j, hop).start()

    def send_piece(j):
        for k in range(NK):
            lt_copy(j, k).start()

        @pl.when(odd == 0)
        def _():
            lt_copy(j, NK).start()

    @pl.when(odd == 1)
    def _():
        for j in range(NP):
            round_copy(j, 0).start()

    send_piece(0)
    for copy in local_copies:
        copy.wait()

    def total(parts):
        x = sum(parts[1:], parts[0])
        x = jnp.sum(x, axis=0, keepdims=True)
        return jnp.broadcast_to(jnp.sum(x, axis=1, keepdims=True), (1, T))

    def merged(parts):
        rows = [[p[i : i + 1] for p in parts] for i in range(7)]
        add = lambda values: sum(values[1:], values[0])
        sizes, means = rows[1], rows[2]
        size = add(sizes)
        weighted = add([m * s for m, s in zip(means, sizes)])
        mean = jnp.where(size > 0.0, weighted / jnp.where(size > 0.0, size, 1.0), 0.0)
        spread = add([s * (m - mean) * (m - mean) for m, s in zip(means, sizes)])
        return [add(rows[0]), size, mean, add(rows[3]) + spread] + [add(r) for r in rows[4:]]

    def copies_of(n, stage, size, me, box, sends, recvs, move, order):
        return [
            pltpu.make_async_remote_copy(
                src_ref=mine.at[n, stage],
                dst_ref=box.at[n, me],
                send_sem=sends.at[n, d],
                recv_sem=recvs.at[n, d],
                device_id=move(d),
                device_id_type=MESH,
            )
            for d in order
        ]

    def stage_y(n):
        return copies_of(n, 0, NY, y, xy, xy_send, xy_recv, lambda d: at(dy=d), (2, 1, 3))

    def stage_z(n):
        order = (4, 3, 5, 2, 6, 1, 7)
        return copies_of(n, 1, NZ, z, xz, xz_send, xz_recv, lambda d: at(dz=d), order)

    def post(n, stage, values, copies, box, me):
        for i, value in enumerate(values):
            mine[n, stage, pl.ds(i, 1), :] = value
        for copy in copies:
            copy.start()
        box[n, me] = mine[n, stage]

    def exchange_open(n, values):
        post(n, 0, values, stage_y(n), xy, y)

    def exchange_pass(n):
        for copy in stage_y(n):
            copy.wait()
        post(n, 1, merged([xy[n, i] for i in range(NY)]), stage_z(n), xz, z)

    def exchange_close(n):
        for copy in stage_z(n):
            copy.wait()
        return merged([xz[n, i] for i in range(NZ)])

    row_at = lax.broadcasted_iota(jnp.int32, (T, T), 0)
    col_at = lax.broadcasted_iota(jnp.int32, (T, T), 1)

    def mask(tile, first, rows):
        return (row_at[:rows] + first < rows_ref[tile]) & (col_at[:rows] < cols_ref[tile])

    def mean_energy(weighted, size):
        value = jnp.where(size > 0.0, weighted / jnp.where(size > 0.0, size, 1.0), 0.0)
        return jnp.clip(value, -2.0, 2.0)

    zero = jnp.zeros((1, T), F32)
    squares = []
    for i in range(NK):
        q = jnp.where(mask(i, 0, T), start_ref[i].astype(F32), 0.0)
        cur[i] = q
        squares.append(q * q)
    weighted = total([square * energy_ref[i] for i, square in enumerate(squares)])
    exchange_open(STEPS, [zero, total(squares), zero, zero, weighted, zero, zero])
    pass_round((0, 1))
    exchange_pass(STEPS)
    send_piece(1)
    pass_round((1, 1))
    _, size, _, _, weighted, _, _ = exchange_close(STEPS)
    scale = lax.rsqrt(size / ENTRIES + EPS)
    shift = mean_energy(weighted, size)
    feeds_left = (seg > 0).astype(F32)
    for i in range(NK):
        q = cur[i] * scale
        cur[i] = q
        prev[i] = jnp.zeros((T, T), F32)
        near[i] = jnp.zeros((T, T), F32)
        low[i] = (q * feeds_left).astype(BF16)
    coef[...] = jnp.zeros((1, T), F32)
    pass_round((2, 1), (0, 2), (3, 1), (1, 2))
    send_piece(2)

    def ring(side, bufs, boxes, sends, recvs, n, me, move):
        far = n // 2

        def parts(up, d):
            if d < far:
                return pl.ds(0, 2)
            return pl.ds(0 if up else 1, 1)

        def copy(j, up, d):
            sign = 1 if up else -1
            goal = lax.rem(me + sign * d + n, n)
            return pltpu.make_async_remote_copy(
                src_ref=bufs[j].at[goal, parts(up, d)],
                dst_ref=boxes[j].at[side, 0 if up else 1, d - 1, parts(up, d)],
                send_sem=sends.at[side * NP + j, 0 if up else 1, d - 1],
                recv_sem=recvs.at[side * NP + j, 0 if up else 1, d - 1],
                device_id=move(sign),
                device_id_type=MESH,
            )

        def step(j, hop):
            d = far - hop
            for up in (True, False):
                if hop > 0:
                    copy(j, up, d + 1).wait_recv()
                    goal = lax.rem(me + (d if up else -d) + n, n)
                    piece = parts(up, d + 1)
                    got = boxes[j][side, 0 if up else 1, d, piece].astype(F32)
                    own = bufs[j][goal, piece].astype(F32)
                    bufs[j][goal, piece] = (own + got).astype(BF16)
                copy(j, up, d).start()

        def last(j, h):
            return [boxes[j][side, i, 0, h] for i in range(2)]

        def arrive(j):
            copy(j, True, 1).wait_recv()
            copy(j, False, 1).wait_recv()

        def drain(j):
            for d in range(1, far + 1):
                copy(j, True, d).wait_send()
                copy(j, False, d).wait_send()

        return step, arrive, last, drain

    def direct(side, bufs, boxes, sends, recvs, n, me, move):
        far = n // 2
        order = sorted(range(1, n), key=lambda d: -min(d, n - d))

        def copy(j, d):
            at_box = ((d - 1) // far, (d - 1) % far)
            return pltpu.make_async_remote_copy(
                src_ref=bufs[j].at[lax.rem(me + d, n)],
                dst_ref=boxes[j].at[(side,) + at_box],
                send_sem=sends.at[(side * NP + j,) + at_box],
                recv_sem=recvs.at[(side * NP + j,) + at_box],
                device_id=move(d),
                device_id_type=MESH,
            )

        def step(j, hop):
            for d in order:
                copy(j, d).start()

        def arrive(j):
            for d in order:
                copy(j, d).wait_recv()

        def last(j, h):
            return [boxes[j][side, (d - 1) // far, (d - 1) % far, h] for d in range(1, n)]

        def drain(j):
            for d in order:
                copy(j, d).wait_send()

        return step, arrive, last, drain

    def relay(side, bufs, boxes, sends, recvs, n, me, move):
        far = n // 2
        rounds = [(up, d) for d in range(far, 0, -1) for up in (True, False)]

        def parts(up, d):
            if d < far:
                return pl.ds(0, 2)
            return pl.ds(0 if up else 1, 1)

        def copy(j, up, d):
            sign = 1 if up else -1
            row = 0 if up else 1
            return pltpu.make_async_remote_copy(
                src_ref=bufs[j].at[lax.rem(me + sign * d + n, n), parts(up, d)],
                dst_ref=boxes[j].at[side, row, d - 1, parts(up, d)],
                send_sem=sends.at[side * NP + j, row, d - 1],
                recv_sem=recvs.at[side * NP + j, row, d - 1],
                device_id=move(sign * max(d - 1, 1)),
                device_id_type=MESH,
            )

        def step(j, hop):
            if hop == 0:
                for up, d in rounds[:-2]:
                    copy(j, up, d).start()
                return
            for up, d in rounds[:-2]:
                copy(j, up, d).wait_recv()
            for up in (True, False):
                row = 0 if up else 1
                goal = lax.rem(me + (1 if up else -1) + n, n)
                for h in range(2):
                    reach = range(2, far + 1 if h == row else far)
                    terms = [boxes[j][side, row, d - 1, h] for d in reach]
                    bufs[j][goal, h] = add([bufs[j][goal, h]] + terms).astype(BF16)
                copy(j, up, 1).start()

        def arrive(j):
            copy(j, True, 1).wait_recv()
            copy(j, False, 1).wait_recv()

        def last(j, h):
            return [boxes[j][side, i, 0, h] for i in range(2)]

        def drain(j):
            for up, d in rounds:
                copy(j, up, d).wait_send()

        return step, arrive, last, drain

    up_z = lambda s: at(dz=s)
    up_y = lambda s: at(dy=s)
    def add(values):
        values = [value.astype(F32) for value in values]
        return sum(values[1:], values[0])

    def turn_over(j, stage, src, me, goals, count, wide):
        _, arrive, last, _ = stage
        arrive(j)
        for h in range(2):
            got = last(j, h)
            for c in range(count):
                for i in range(wide):
                    value = add([src[j][me, h, c, i]] + [g[c, i] for g in got])
                    goals[j][i, h, c] = value.astype(BF16)

    def image(j, tile, h, value):
        first = j * PR + h * HR
        img[tile, pl.ds(first, HR)] = jnp.where(mask(tile, first, HR), value, 0.0)

    def into_image(j, stage, src, me, count, first_tile):
        _, arrive, last, _ = stage
        arrive(j)
        for h in range(2):
            got = last(j, h)
            for c in range(count):
                image(j, first_tile + c, h, add([src[j][me, h, c]] + [g[c] for g in got]))

    def network(side):
        a1 = ring(side, qa, ra, a1_send, a1_recv, NZ, z, up_z)
        b1 = ring(side, qb, rb, b1_send, b1_recv, NY, y, up_y)
        a2_args = (side, sa, rsa, a2_send, a2_recv, NY, y, up_y)
        b2_args = (side, sb, rsb, b2_send, b2_recv, NZ, z, up_z)
        a2_of = [(direct if flag else ring)(*a2_args) for flag in A2_DIRECT]
        b2_of = [{1: direct, 2: relay, 4: ring}[r](*b2_args) for r in B2_ROUNDS]

        def a_life(j):
            events = [functools.partial(a1[0], j, hop) for hop in range(NZ // 2)]

            def turn():
                turn_over(j, a1, qa, z, sa, NA[j], NY)
                a2_of[j][0](j, 0)

            events.append(turn)
            if not A2_DIRECT[j]:
                events += [functools.partial(a2_of[j][0], j, hop) for hop in range(1, NY // 2)]
            events.append(lambda: into_image(j, a2_of[j], sa, y, NA[j], 0))
            return events

        def b_life(j):
            events = [functools.partial(b1[0], j, hop) for hop in range(NY // 2)]

            def turn():
                turn_over(j, b1, qb, y, sb, NK - NA[j], NZ)
                b2_of[j][0](j, 0)

            events.append(turn)
            events += [functools.partial(b2_of[j][0], j, hop) for hop in range(1, B2_ROUNDS[j])]
            events.append(lambda: into_image(j, b2_of[j], sb, z, NK - NA[j], NA[j]))
            return events

        lives = [(a_life(j), b_life(j)) for j in range(NP)]
        life_of = [max(len(a), len(b)) for a, b in lives]

        def play(j, n):
            for life in lives[j]:
                if 0 <= n < len(life):
                    life[n]()

        def drain():
            for j in range(NP):
                for stage in (a1, b1, a2_of[j], b2_of[j]):
                    stage[3](j)

        return play, drain, max(life_of)

    networks = [network(0), network(1)]

    CH = 17
    UN = 8

    def contributions(first, count):
        rows = count * PR

        def left_body(i, carry):
            for c in range(count):
                for s in range(2):
                    slot = pl.multiple_of(i * CH, CH) + s * (2 * NW)
                    k = lax.div(i * CH, NW) + 2 * s
                    tiles = lt[first + c, pl.ds(slot, CH)].reshape(CH * PR, T)
                    value = jnp.dot(tiles, low[k], preferred_element_type=F32).astype(BF16)
                    half[pl.ds(slot, CH), pl.ds(c * PR, PR)] = value.reshape(CH, PR, T)
            return carry

        lax.fori_loop(0, NS // (2 * CH), left_body, 0)

        def right_body(i, acc):
            values = []
            for n in range(UN):
                slot = order_ref[i * UN + n]
                values.append(
                    jnp.dot(half[slot, pl.ds(0, rows)], rt[slot], preferred_element_type=F32)
                )
            for n in range(UN):
                here = i * UN + n
                before = jnp.maximum(here - 1, 0)
                same = goal_ref[here] == goal_ref[before]
                acc = jnp.where(same, acc, 0.0) + values[n]
                run[here, pl.ds(0, rows)] = acc.astype(BF16)
            return acc

        lax.fori_loop(0, NS // UN, right_body, jnp.zeros((rows, T), F32))

        def pick(o, carry):
            zo, yo = lax.div(o, NY), lax.rem(o, NY)
            for tile in range(NK):
                t = o * NK + tile
                value = run[last_ref[t], pl.ds(0, rows)]
                value = jnp.where(has_ref[t] > 0, value, jnp.zeros_like(value))
                for c in range(count):
                    for h in range(2):
                        part = value[c * PR + h * HR : c * PR + (h + 1) * HR]
                        j = first + c
                        if tile < NA[j]:
                            qa[j][zo, h, tile, yo] = part
                        else:
                            qb[j][yo, h, tile - NA[j], zo] = part
            return carry

        lax.fori_loop(0, NBLK, pick, 0)

    def settle(extra, scale, beta, shift):
        for i in range(NK):
            n_q = img[i]
            if scale is not None:
                n_q = (n_q - extra * near[i]) * scale
            near[i] = n_q
            g = n_q + (energy_ref[i] - shift) * cur[i] - beta * prev[i]
            ahead[i] = g
            low[i] = (g * feeds_left).astype(BF16)

    def sums(shift):
        dots, sizes, alongs, ones, twos, threes = [], [], [], [], [], []
        for i in range(NK):
            q, w, e = cur[i], ahead[i], energy_ref[i]
            dots.append(q * (near[i] + e * q))
            sizes.append(q * q)
            alongs.append(q * w)
            ones.append(e * (w * w))
            twos.append(e * (w * q))
            threes.append(e * (q * q))
        size, along = total(sizes), total(alongs)
        mean = jnp.where(size > 0.0, along / jnp.where(size > 0.0, size, 1.0), 0.0)
        rests = []
        for i in range(NK):
            rest = ahead[i] - mean * cur[i]
            rests.append(rest * rest)
        return [
            total(dots), size, mean, total(rests), total(ones), total(twos), total(threes),
        ]

    def conclude(n, shift):
        dot, size, mean, rest, one, two, three = exchange_close(n)
        alpha = dot / ENTRIES
        extra = alpha - shift
        whole = rest + size * (mean - extra) * (mean - extra)
        square = whole / ENTRIES
        beta = jnp.sqrt(square)
        lane = lax.broadcasted_iota(jnp.int32, (1, T), 1)
        value = jnp.where(lane == n, alpha, coef[...])
        coef[...] = jnp.where(lane == n + STEPS, beta, value)
        next_shift = mean_energy(one - 2.0 * extra * two + extra * extra * three, whole)
        return extra, lax.rsqrt(square + EPS), beta, next_shift

    play, drain, turns = networks[0]
    for j in range(NP):
        for i in range(j):
            play(i, 2 * (j - i) - 1)
        for k in range(NK + 1):
            lt_copy(j, k).wait_recv()
        contributions(j, 1)
        for i in range(j + 1):
            play(i, 2 * (j - i))
        if j == 0:
            pass_round((2, 2), (3, 2))
            send_piece(3)
    for turn in range(1, turns):
        for j in range(NP):
            play(j, 2 * (NP - 1 - j) + turn)
    drain()
    for j in range(NP):
        for k in range(NK):
            lt_copy(j, k).wait_send()

        @pl.when(odd == 1)
        def _():
            for hop in range(3):
                round_copy(j, hop).wait_send()

        @pl.when(odd == 0)
        def _():
            lt_copy(j, NK).wait_send()

    settle(None, None, zero, shift)

    for n in range(1, STEPS):
        play, drain, turns = networks[n % 2]
        contributions(0, NP)
        for j in range(NP):
            play(j, 0)
        exchange_open(n - 1, sums(shift))
        extra = scale = beta = None
        for turn in range(1, turns):
            for j in range(NP):
                play(j, turn)
            if turn == 1:
                exchange_pass(n - 1)
            if turn == 3:
                extra, scale, beta, next_shift = conclude(n - 1, shift)
                shift = next_shift
                for i in range(NK):
                    q = cur[i]
                    prev[i] = q
                    cur[i] = (ahead[i] - extra * q) * scale
        drain()
        settle(extra, scale, beta, shift)
    exchange_open(STEPS - 1, sums(shift))
    exchange_pass(STEPS - 1)
    extra, _, _, _ = conclude(STEPS - 1, shift)
    for i in range(NK):
        out_ref[i] = ahead[i] - extra * cur[i]
    coef_ref[...] = coef[:, : 2 * STEPS]


def local(start, left, right, energy, rows, cols, feeds):
    feeds = feeds.reshape(NS)
    slots = jnp.arange(NS, dtype=jnp.int32)
    ahead = (feeds[None, :] < feeds[:, None]) | (
        (feeds[None, :] == feeds[:, None]) & (slots[None, :] < slots[:, None])
    )
    rank = jnp.sum(ahead.astype(jnp.int32), axis=1)
    here = rank[:, None] == slots[None, :]
    order = jnp.sum(jnp.where(here, slots[:, None], 0), axis=0)
    goal = jnp.sum(jnp.where(here, feeds[:, None], 0), axis=0)
    targets = jnp.arange(NT, dtype=jnp.int32)
    upto = jnp.sum((feeds[:, None] <= targets[None, :]).astype(jnp.int32), axis=0)
    has = jnp.sum((feeds[:, None] == targets[None, :]).astype(jnp.int32), axis=0)
    last = jnp.maximum(upto - 1, 0)

    vmem = pl.BlockSpec(memory_space=pltpu.VMEM)
    hbm = pl.BlockSpec(memory_space=pl.ANY)
    dma = pltpu.SemaphoreType.DMA

    def piecewise(shape):
        return [pltpu.VMEM(shape(na, NK - na), BF16) for na in NA]

    coef, residual = pl.pallas_call(
        kernel,
        out_shape=(
            jax.ShapeDtypeStruct((1, 2 * STEPS), F32),
            jax.ShapeDtypeStruct((NK, T, T), F32),
        ),
        in_specs=[hbm] * 10,
        out_specs=(vmem, vmem),
        scratch_shapes=[
            pltpu.VMEM((NK, T, T), BF16),
            [pltpu.SMEM((NK,), F32)]
            + [pltpu.SMEM((size,), jnp.int32) for size in (NK, NK, NS, NS, NT, NT)],
            dma((8,)),
            pltpu.VMEM((NP, NS, PR, T), BF16),
            pltpu.VMEM((NS, T, T), BF16),
            pltpu.VMEM((NS, T, T), BF16),
            pltpu.VMEM((NS, T, T), BF16),
            piecewise(lambda na, nb: (NZ, 2, na, NY, HR, T)),
            piecewise(lambda na, nb: (NY, 2, nb, NZ, HR, T)),
            piecewise(lambda na, nb: (NY, 2, na, HR, T)),
            piecewise(lambda na, nb: (NZ, 2, nb, HR, T)),
            piecewise(lambda na, nb: (2, 2, NZ // 2, 2, na, NY, HR, T)),
            piecewise(lambda na, nb: (2, 2, NY // 2, 2, nb, NZ, HR, T)),
            piecewise(lambda na, nb: (2, 2, NY // 2, 2, na, HR, T)),
            piecewise(lambda na, nb: (2, 2, NZ // 2, 2, nb, HR, T)),
            pltpu.VMEM((NK, T, T), F32),
            pltpu.VMEM((NK, T, T), F32),
            pltpu.VMEM((NK, T, T), F32),
            pltpu.VMEM((NK, T, T), F32),
            pltpu.VMEM((NK, T, T), F32),
            pltpu.VMEM((NK, T, T), BF16),
            pltpu.VMEM((1, T), F32),
            pltpu.VMEM((STEPS + 1, 2, 8, T), F32),
            pltpu.VMEM((STEPS + 1, NY, 8, T), F32),
            pltpu.VMEM((STEPS + 1, NZ, 8, T), F32),
            dma((NP, NK + 1)),
            dma((NP, NK + 1)),
            pltpu.VMEM((2, NP, NX, PR, T), BF16),
            dma((3, NP)),
            dma((3, NP)),
            dma,
            dma((2 * NP, 2, NZ // 2)),
            dma((2 * NP, 2, NZ // 2)),
            dma((2 * NP, 2, NY // 2)),
            dma((2 * NP, 2, NY // 2)),
            dma((2 * NP, 2, NY // 2)),
            dma((2 * NP, 2, NY // 2)),
            dma((2 * NP, 2, NZ // 2)),
            dma((2 * NP, 2, NZ // 2)),
            dma((STEPS + 1, NY)),
            dma((STEPS + 1, NY)),
            dma((STEPS + 1, NZ)),
            dma((STEPS + 1, NZ)),
        ],
        compiler_params=pltpu.CompilerParams(
            collective_id=0, has_side_effects=True, vmem_limit_bytes=60 * 2**20
        ),
        cost_estimate=pl.CostEstimate(
            flops=STEPS * NS * 4 * T**3, bytes_accessed=4 * NS * T * T, transcendentals=0
        ),
        name="lanczos",
    )(
        start[0],
        left[0],
        right[0].reshape(NS, T, T),
        energy[0],
        rows[0],
        cols[0],
        order,
        goal,
        last,
        has,
    )
    return coef, residual[None]


def solution(mesh):
    return jax.shard_map(
        local,
        mesh=mesh,
        in_specs=(
            P("seg", "blk", None, None),
            P("seg", "blk", None, None, None),
            P("seg", "blk", None, None, None),
            P("seg", "blk"),
            P("seg", "blk"),
            P("seg", "blk"),
            P("seg", "blk", None),
        ),
        out_specs=(P("seg", None), P("seg", "blk", None, None)),
        check_vma=False,
    )
```

```python
import functools

import jax
import jax.numpy as jnp
from jax import lax
from jax.experimental import pallas as pl
from jax.experimental.pallas import tpu as pltpu
from jax.sharding import PartitionSpec as P

STEPS = 3
EPS = 1e-06
T = 128
NK = 4
NW = 34
NS = NK * NW
NZ, NY = 8, 4
NBLK = NZ * NY
NSEG = 8
NT = NK * NBLK
PR = 32
NP = T // PR
HR = PR // 2
NX = 14
NA = (2, 2, 1, 1)
A2_DIRECT = (True,) * NP
B2_ROUNDS = (2, 2, 2, 2)
ENTRIES = float(NT * T * T)
F32 = jnp.float32
BF16 = jnp.bfloat16
MESH = pl.DeviceIdType.MESH


def kernel(
    start_hbm,
    left_ref,
    right_ref,
    energy_hbm,
    rows_hbm,
    cols_hbm,
    order_hbm,
    goal_hbm,
    last_hbm,
    has_hbm,
    coef_ref,
    out_ref,
    start_ref,
    scalars,
    scalar_sem,
    lt,
    rt,
    half,
    run,
    qa,
    qb,
    sa,
    sb,
    ra,
    rb,
    rsa,
    rsb,
    cur,
    prev,
    img,
    near,
    ahead,
    low,
    coef,
    mine,
    xy,
    xz,
    lt_send,
    lt_recv,
    round_box,
    round_send,
    round_recv,
    rt_sem,
    a1_send,
    a1_recv,
    a2_send,
    a2_recv,
    b1_send,
    b1_recv,
    b2_send,
    b2_recv,
    xy_send,
    xy_recv,
    xz_send,
    xz_recv,
):
    seg = lax.axis_index("seg")
    blk = lax.axis_index("blk")
    z = blk // NY
    y = blk % NY

    def at(dz=0, dy=0, ds=0):
        zz = lax.rem(z + dz + NZ, NZ)
        yy = lax.rem(y + dy + NY, NY)
        return (lax.rem(seg + ds + NSEG, NSEG), zz * NY + yy)

    barrier = pltpu.get_barrier_semaphore()
    peers = [at(ds=1), at(ds=-1)]
    peers += [at(dz=d) for d in (4, 3, 5, 2, 6, 1, 7)] + [at(dy=d) for d in (2, 1, 3)]
    for peer in peers:
        pl.semaphore_signal(barrier, inc=1, device_id=peer, device_id_type=MESH)
    odd = lax.rem(seg, 2)

    @pl.when(odd == 1)
    def _():
        for ds in (2, -2, -3):
            pl.semaphore_signal(barrier, inc=1, device_id=at(ds=ds), device_id_type=MESH)

    @pl.when(odd == 0)
    def _():
        pl.semaphore_signal(barrier, inc=1, device_id=at(ds=3), device_id_type=MESH)

    energy_ref, rows_ref, cols_ref, order_ref, goal_ref, last_ref, has_ref = scalars
    local_copies = [pltpu.make_async_copy(start_hbm, start_ref, scalar_sem.at[7])]
    sources = (energy_hbm, rows_hbm, cols_hbm, order_hbm, goal_hbm, last_hbm, has_hbm)
    for i, (source, goal) in enumerate(zip(sources, scalars)):
        local_copies.append(pltpu.make_async_copy(source, goal, scalar_sem.at[i]))
    local_copies.append(pltpu.make_async_copy(right_ref, rt, rt_sem))
    for copy in local_copies:
        copy.start()
    pl.semaphore_wait(barrier, len(peers) + 1 + 2 * odd)

    def lt_copy(j, k):
        tile = min(k, NK - 1)
        first, count = ((0, NW), (0, NW - NX), (NW - NX, NX))[max(k - NK + 2, 0)]
        return pltpu.make_async_remote_copy(
            src_ref=left_ref.at[tile, pl.ds(first, count), pl.ds(j * PR, PR), :],
            dst_ref=lt.at[j, pl.ds(tile * NW + first, count)],
            send_sem=lt_send.at[j, k],
            recv_sem=lt_recv.at[j, k],
            device_id=at(ds=1),
            device_id_type=MESH,
        )

    def round_copy(j, hop):
        source = left_ref.at[NK - 1, pl.ds(NW - NX, NX), pl.ds(j * PR, PR), :]
        return pltpu.make_async_remote_copy(
            src_ref=source if hop == 0 else round_box.at[hop - 1, j],
            dst_ref=lt.at[j, pl.ds(NS - NX, NX)] if hop == 2 else round_box.at[hop, j],
            send_sem=round_send.at[hop, j],
            recv_sem=lt_recv.at[j, NK] if hop == 2 else round_recv.at[hop, j],
            device_id=at(ds=-3) if hop == 2 else at(ds=-2),
            device_id_type=MESH,
        )

    def pass_round(*moves):
        @pl.when(odd == 1)
        def _():
            for j, hop in moves:
                round_copy(j, hop - 1).wait_recv()
                round_copy(j, hop).start()

    def send_piece(j):
        for k in range(NK):
            lt_copy(j, k).start()

        @pl.when(odd == 0)
        def _():
            lt_copy(j, NK).start()

    @pl.when(odd == 1)
    def _():
        for j in range(NP):
            round_copy(j, 0).start()

    send_piece(0)
    for copy in local_copies:
        copy.wait()

    def total(parts):
        x = sum(parts[1:], parts[0])
        x = jnp.sum(x, axis=0, keepdims=True)
        return jnp.broadcast_to(jnp.sum(x, axis=1, keepdims=True), (1, T))

    def merged(parts):
        rows = [[p[i : i + 1] for p in parts] for i in range(7)]
        add = lambda values: sum(values[1:], values[0])
        sizes, means = rows[1], rows[2]
        size = add(sizes)
        weighted = add([m * s for m, s in zip(means, sizes)])
        mean = jnp.where(size > 0.0, weighted / jnp.where(size > 0.0, size, 1.0), 0.0)
        spread = add([s * (m - mean) * (m - mean) for m, s in zip(means, sizes)])
        return [add(rows[0]), size, mean, add(rows[3]) + spread] + [add(r) for r in rows[4:]]

    def copies_of(n, stage, size, me, box, sends, recvs, move, order):
        return [
            pltpu.make_async_remote_copy(
                src_ref=mine.at[n, stage],
                dst_ref=box.at[n, me],
                send_sem=sends.at[n, d],
                recv_sem=recvs.at[n, d],
                device_id=move(d),
                device_id_type=MESH,
            )
            for d in order
        ]

    def stage_y(n):
        return copies_of(n, 0, NY, y, xy, xy_send, xy_recv, lambda d: at(dy=d), (2, 1, 3))

    def stage_z(n):
        order = (4, 3, 5, 2, 6, 1, 7)
        return copies_of(n, 1, NZ, z, xz, xz_send, xz_recv, lambda d: at(dz=d), order)

    def post(n, stage, values, copies, box, me):
        for i, value in enumerate(values):
            mine[n, stage, pl.ds(i, 1), :] = value
        for copy in copies:
            copy.start()
        box[n, me] = mine[n, stage]

    def exchange_open(n, values):
        post(n, 0, values, stage_y(n), xy, y)

    def exchange_pass(n):
        for copy in stage_y(n):
            copy.wait()
        post(n, 1, merged([xy[n, i] for i in range(NY)]), stage_z(n), xz, z)

    def exchange_close(n):
        for copy in stage_z(n):
            copy.wait()
        return merged([xz[n, i] for i in range(NZ)])

    row_at = lax.broadcasted_iota(jnp.int32, (T, T), 0)
    col_at = lax.broadcasted_iota(jnp.int32, (T, T), 1)

    def mask(tile, first, rows):
        return (row_at[:rows] + first < rows_ref[tile]) & (col_at[:rows] < cols_ref[tile])

    def mean_energy(weighted, size):
        value = jnp.where(size > 0.0, weighted / jnp.where(size > 0.0, size, 1.0), 0.0)
        return jnp.clip(value, -2.0, 2.0)

    zero = jnp.zeros((1, T), F32)
    squares = []
    for i in range(NK):
        q = jnp.where(mask(i, 0, T), start_ref[i].astype(F32), 0.0)
        cur[i] = q
        squares.append(q * q)
    weighted = total([square * energy_ref[i] for i, square in enumerate(squares)])
    exchange_open(STEPS, [zero, total(squares), zero, zero, weighted, zero, zero])
    pass_round((0, 1))
    exchange_pass(STEPS)
    send_piece(1)
    pass_round((1, 1))
    _, size, _, _, weighted, _, _ = exchange_close(STEPS)
    scale = lax.rsqrt(size / ENTRIES + EPS)
    shift = mean_energy(weighted, size)
    feeds_left = (seg > 0).astype(F32)
    for i in range(NK):
        q = cur[i] * scale
        cur[i] = q
        prev[i] = jnp.zeros((T, T), F32)
        near[i] = jnp.zeros((T, T), F32)
        low[i] = (q * feeds_left).astype(BF16)
    coef[...] = jnp.zeros((1, T), F32)
    pass_round((2, 1), (0, 2), (3, 1), (1, 2))
    send_piece(2)

    def ring(side, bufs, boxes, sends, recvs, n, me, move):
        far = n // 2

        def parts(up, d):
            if d < far:
                return pl.ds(0, 2)
            return pl.ds(0 if up else 1, 1)

        def copy(j, up, d):
            sign = 1 if up else -1
            goal = lax.rem(me + sign * d + n, n)
            return pltpu.make_async_remote_copy(
                src_ref=bufs[j].at[goal, parts(up, d)],
                dst_ref=boxes[j].at[side, 0 if up else 1, d - 1, parts(up, d)],
                send_sem=sends.at[side * NP + j, 0 if up else 1, d - 1],
                recv_sem=recvs.at[side * NP + j, 0 if up else 1, d - 1],
                device_id=move(sign),
                device_id_type=MESH,
            )

        def step(j, hop):
            d = far - hop
            for up in (True, False):
                if hop > 0:
                    copy(j, up, d + 1).wait_recv()
                    goal = lax.rem(me + (d if up else -d) + n, n)
                    piece = parts(up, d + 1)
                    got = boxes[j][side, 0 if up else 1, d, piece].astype(F32)
                    own = bufs[j][goal, piece].astype(F32)
                    bufs[j][goal, piece] = (own + got).astype(BF16)
                copy(j, up, d).start()

        def last(j, h):
            return [boxes[j][side, i, 0, h] for i in range(2)]

        def arrive(j):
            copy(j, True, 1).wait_recv()
            copy(j, False, 1).wait_recv()

        def drain(j):
            for d in range(1, far + 1):
                copy(j, True, d).wait_send()
                copy(j, False, d).wait_send()

        return step, arrive, last, drain

    def direct(side, bufs, boxes, sends, recvs, n, me, move):
        far = n // 2
        order = sorted(range(1, n), key=lambda d: -min(d, n - d))

        def copy(j, d):
            at_box = ((d - 1) // far, (d - 1) % far)
            return pltpu.make_async_remote_copy(
                src_ref=bufs[j].at[lax.rem(me + d, n)],
                dst_ref=boxes[j].at[(side,) + at_box],
                send_sem=sends.at[(side * NP + j,) + at_box],
                recv_sem=recvs.at[(side * NP + j,) + at_box],
                device_id=move(d),
                device_id_type=MESH,
            )

        def step(j, hop):
            for d in order:
                copy(j, d).start()

        def arrive(j):
            for d in order:
                copy(j, d).wait_recv()

        def last(j, h):
            return [boxes[j][side, (d - 1) // far, (d - 1) % far, h] for d in range(1, n)]

        def drain(j):
            for d in order:
                copy(j, d).wait_send()

        return step, arrive, last, drain

    def relay(side, bufs, boxes, sends, recvs, n, me, move):
        far = n // 2
        rounds = [(up, d) for d in range(far, 0, -1) for up in (True, False)]

        def parts(up, d):
            if d < far:
                return pl.ds(0, 2)
            return pl.ds(0 if up else 1, 1)

        def copy(j, up, d):
            sign = 1 if up else -1
            row = 0 if up else 1
            return pltpu.make_async_remote_copy(
                src_ref=bufs[j].at[lax.rem(me + sign * d + n, n), parts(up, d)],
                dst_ref=boxes[j].at[side, row, d - 1, parts(up, d)],
                send_sem=sends.at[side * NP + j, row, d - 1],
                recv_sem=recvs.at[side * NP + j, row, d - 1],
                device_id=move(sign * max(d - 1, 1)),
                device_id_type=MESH,
            )

        def step(j, hop):
            if hop == 0:
                for up, d in rounds[:-2]:
                    copy(j, up, d).start()
                return
            for up, d in rounds[:-2]:
                copy(j, up, d).wait_recv()
            for up in (True, False):
                row = 0 if up else 1
                goal = lax.rem(me + (1 if up else -1) + n, n)
                for h in range(2):
                    reach = range(2, far + 1 if h == row else far)
                    terms = [boxes[j][side, row, d - 1, h] for d in reach]
                    bufs[j][goal, h] = add([bufs[j][goal, h]] + terms).astype(BF16)
                copy(j, up, 1).start()

        def arrive(j):
            copy(j, True, 1).wait_recv()
            copy(j, False, 1).wait_recv()

        def last(j, h):
            return [boxes[j][side, i, 0, h] for i in range(2)]

        def drain(j):
            for up, d in rounds:
                copy(j, up, d).wait_send()

        return step, arrive, last, drain

    up_z = lambda s: at(dz=s)
    up_y = lambda s: at(dy=s)
    def add(values):
        values = [value.astype(F32) for value in values]
        return sum(values[1:], values[0])

    def turn_over(j, stage, src, me, goals, count, wide):
        _, arrive, last, _ = stage
        arrive(j)
        for h in range(2):
            got = last(j, h)
            for c in range(count):
                for i in range(wide):
                    value = add([src[j][me, h, c, i]] + [g[c, i] for g in got])
                    goals[j][i, h, c] = value.astype(BF16)

    def image(j, tile, h, value):
        first = j * PR + h * HR
        img[tile, pl.ds(first, HR)] = jnp.where(mask(tile, first, HR), value, 0.0)

    def into_image(j, stage, src, me, count, first_tile):
        _, arrive, last, _ = stage
        arrive(j)
        for h in range(2):
            got = last(j, h)
            for c in range(count):
                image(j, first_tile + c, h, add([src[j][me, h, c]] + [g[c] for g in got]))

    def network(side):
        a1 = ring(side, qa, ra, a1_send, a1_recv, NZ, z, up_z)
        b1 = ring(side, qb, rb, b1_send, b1_recv, NY, y, up_y)
        a2_args = (side, sa, rsa, a2_send, a2_recv, NY, y, up_y)
        b2_args = (side, sb, rsb, b2_send, b2_recv, NZ, z, up_z)
        a2_of = [(direct if flag else ring)(*a2_args) for flag in A2_DIRECT]
        b2_of = [{1: direct, 2: relay, 4: ring}[r](*b2_args) for r in B2_ROUNDS]

        def a_life(j):
            events = [functools.partial(a1[0], j, hop) for hop in range(NZ // 2)]

            def turn():
                turn_over(j, a1, qa, z, sa, NA[j], NY)
                a2_of[j][0](j, 0)

            events.append(turn)
            if not A2_DIRECT[j]:
                events += [functools.partial(a2_of[j][0], j, hop) for hop in range(1, NY // 2)]
            events.append(lambda: into_image(j, a2_of[j], sa, y, NA[j], 0))
            return events

        def b_life(j):
            events = [functools.partial(b1[0], j, hop) for hop in range(NY // 2)]

            def turn():
                turn_over(j, b1, qb, y, sb, NK - NA[j], NZ)
                b2_of[j][0](j, 0)

            events.append(turn)
            events += [functools.partial(b2_of[j][0], j, hop) for hop in range(1, B2_ROUNDS[j])]
            events.append(lambda: into_image(j, b2_of[j], sb, z, NK - NA[j], NA[j]))
            return events

        lives = [(a_life(j), b_life(j)) for j in range(NP)]
        life_of = [max(len(a), len(b)) for a, b in lives]

        def play(j, n):
            for life in lives[j]:
                if 0 <= n < len(life):
                    life[n]()

        def drain():
            for j in range(NP):
                for stage in (a1, b1, a2_of[j], b2_of[j]):
                    stage[3](j)

        return play, drain, max(life_of)

    networks = [network(0), network(1)]

    CH = 17
    UN = 17

    def contributions(first, count):
        rows = count * PR

        def left_body(i, carry):
            for c in range(count):
                for s in range(2):
                    slot = pl.multiple_of(i * CH, CH) + s * (2 * NW)
                    k = lax.div(i * CH, NW) + 2 * s
                    tiles = lt[first + c, pl.ds(slot, CH)].reshape(CH * PR, T)
                    value = jnp.dot(tiles, low[k], preferred_element_type=F32).astype(BF16)
                    half[pl.ds(slot, CH), pl.ds(c * PR, PR)] = value.reshape(CH, PR, T)
            return carry

        lax.fori_loop(0, NS // (2 * CH), left_body, 0)

        def right_body(i, acc):
            values = []
            for n in range(UN):
                slot = order_ref[i * UN + n]
                values.append(
                    jnp.dot(half[slot, pl.ds(0, rows)], rt[slot], preferred_element_type=F32)
                )
            for n in range(UN):
                here = i * UN + n
                before = jnp.maximum(here - 1, 0)
                same = goal_ref[here] == goal_ref[before]
                acc = jnp.where(same, acc, 0.0) + values[n]
                run[here, pl.ds(0, rows)] = acc.astype(BF16)
            return acc

        lax.fori_loop(0, NS // UN, right_body, jnp.zeros((rows, T), F32))

        def pick(o, carry):
            zo, yo = lax.div(o, NY), lax.rem(o, NY)
            for tile in range(NK):
                t = o * NK + tile
                value = run[last_ref[t], pl.ds(0, rows)]
                value = jnp.where(has_ref[t] > 0, value, jnp.zeros_like(value))
                for c in range(count):
                    for h in range(2):
                        part = value[c * PR + h * HR : c * PR + (h + 1) * HR]
                        j = first + c
                        if tile < NA[j]:
                            qa[j][zo, h, tile, yo] = part
                        else:
                            qb[j][yo, h, tile - NA[j], zo] = part
            return carry

        lax.fori_loop(0, NBLK, pick, 0)

    def settle(extra, scale, beta, shift):
        for i in range(NK):
            n_q = img[i]
            if scale is not None:
                n_q = (n_q - extra * near[i]) * scale
            near[i] = n_q
            g = n_q + (energy_ref[i] - shift) * cur[i] - beta * prev[i]
            ahead[i] = g
            low[i] = (g * feeds_left).astype(BF16)

    def sums(shift):
        dots, sizes, alongs, ones, twos, threes = [], [], [], [], [], []
        for i in range(NK):
            q, w, e = cur[i], ahead[i], energy_ref[i]
            dots.append(q * (near[i] + e * q))
            sizes.append(q * q)
            alongs.append(q * w)
            ones.append(e * (w * w))
            twos.append(e * (w * q))
            threes.append(e * (q * q))
        size, along = total(sizes), total(alongs)
        mean = jnp.where(size > 0.0, along / jnp.where(size > 0.0, size, 1.0), 0.0)
        rests = []
        for i in range(NK):
            rest = ahead[i] - mean * cur[i]
            rests.append(rest * rest)
        return [
            total(dots), size, mean, total(rests), total(ones), total(twos), total(threes),
        ]

    def conclude(n, shift):
        dot, size, mean, rest, one, two, three = exchange_close(n)
        alpha = dot / ENTRIES
        extra = alpha - shift
        whole = rest + size * (mean - extra) * (mean - extra)
        square = whole / ENTRIES
        beta = jnp.sqrt(square)
        lane = lax.broadcasted_iota(jnp.int32, (1, T), 1)
        value = jnp.where(lane == n, alpha, coef[...])
        coef[...] = jnp.where(lane == n + STEPS, beta, value)
        next_shift = mean_energy(one - 2.0 * extra * two + extra * extra * three, whole)
        return extra, lax.rsqrt(square + EPS), beta, next_shift

    play, drain, turns = networks[0]
    for j in range(NP):
        for i in range(j):
            play(i, 2 * (j - i) - 1)
        for k in range(NK + 1):
            lt_copy(j, k).wait_recv()
        contributions(j, 1)
        for i in range(j + 1):
            play(i, 2 * (j - i))
        if j == 0:
            pass_round((2, 2), (3, 2))
            send_piece(3)
    for turn in range(1, turns):
        for j in range(NP):
            play(j, 2 * (NP - 1 - j) + turn)
    drain()
    for j in range(NP):
        for k in range(NK):
            lt_copy(j, k).wait_send()

        @pl.when(odd == 1)
        def _():
            for hop in range(3):
                round_copy(j, hop).wait_send()

        @pl.when(odd == 0)
        def _():
            lt_copy(j, NK).wait_send()

    settle(None, None, zero, shift)

    for n in range(1, STEPS):
        play, drain, turns = networks[n % 2]
        contributions(0, NP)
        for j in range(NP):
            play(j, 0)
        exchange_open(n - 1, sums(shift))
        extra = scale = beta = None
        for turn in range(1, turns):
            for j in range(NP):
                play(j, turn)
            if turn == 1:
                exchange_pass(n - 1)
            if turn == 3:
                extra, scale, beta, next_shift = conclude(n - 1, shift)
                shift = next_shift
                for i in range(NK):
                    q = cur[i]
                    prev[i] = q
                    cur[i] = (ahead[i] - extra * q) * scale
        drain()
        settle(extra, scale, beta, shift)
    exchange_open(STEPS - 1, sums(shift))
    exchange_pass(STEPS - 1)
    extra, _, _, _ = conclude(STEPS - 1, shift)
    for i in range(NK):
        out_ref[i] = ahead[i] - extra * cur[i]
    coef_ref[...] = coef[:, : 2 * STEPS]


def local(start, left, right, energy, rows, cols, feeds):
    feeds = feeds.reshape(NS)
    slots = jnp.arange(NS, dtype=jnp.int32)
    ahead = (feeds[None, :] < feeds[:, None]) | (
        (feeds[None, :] == feeds[:, None]) & (slots[None, :] < slots[:, None])
    )
    rank = jnp.sum(ahead.astype(jnp.int32), axis=1)
    here = rank[:, None] == slots[None, :]
    order = jnp.sum(jnp.where(here, slots[:, None], 0), axis=0)
    goal = jnp.sum(jnp.where(here, feeds[:, None], 0), axis=0)
    targets = jnp.arange(NT, dtype=jnp.int32)
    upto = jnp.sum((feeds[:, None] <= targets[None, :]).astype(jnp.int32), axis=0)
    has = jnp.sum((feeds[:, None] == targets[None, :]).astype(jnp.int32), axis=0)
    last = jnp.maximum(upto - 1, 0)

    vmem = pl.BlockSpec(memory_space=pltpu.VMEM)
    hbm = pl.BlockSpec(memory_space=pl.ANY)
    dma = pltpu.SemaphoreType.DMA

    def piecewise(shape):
        return [pltpu.VMEM(shape(na, NK - na), BF16) for na in NA]

    coef, residual = pl.pallas_call(
        kernel,
        out_shape=(
            jax.ShapeDtypeStruct((1, 2 * STEPS), F32),
            jax.ShapeDtypeStruct((NK, T, T), F32),
        ),
        in_specs=[hbm] * 10,
        out_specs=(vmem, vmem),
        scratch_shapes=[
            pltpu.VMEM((NK, T, T), BF16),
            [pltpu.SMEM((NK,), F32)]
            + [pltpu.SMEM((size,), jnp.int32) for size in (NK, NK, NS, NS, NT, NT)],
            dma((8,)),
            pltpu.VMEM((NP, NS, PR, T), BF16),
            pltpu.VMEM((NS, T, T), BF16),
            pltpu.VMEM((NS, T, T), BF16),
            pltpu.VMEM((NS, T, T), BF16),
            piecewise(lambda na, nb: (NZ, 2, na, NY, HR, T)),
            piecewise(lambda na, nb: (NY, 2, nb, NZ, HR, T)),
            piecewise(lambda na, nb: (NY, 2, na, HR, T)),
            piecewise(lambda na, nb: (NZ, 2, nb, HR, T)),
            piecewise(lambda na, nb: (2, 2, NZ // 2, 2, na, NY, HR, T)),
            piecewise(lambda na, nb: (2, 2, NY // 2, 2, nb, NZ, HR, T)),
            piecewise(lambda na, nb: (2, 2, NY // 2, 2, na, HR, T)),
            piecewise(lambda na, nb: (2, 2, NZ // 2, 2, nb, HR, T)),
            pltpu.VMEM((NK, T, T), F32),
            pltpu.VMEM((NK, T, T), F32),
            pltpu.VMEM((NK, T, T), F32),
            pltpu.VMEM((NK, T, T), F32),
            pltpu.VMEM((NK, T, T), F32),
            pltpu.VMEM((NK, T, T), BF16),
            pltpu.VMEM((1, T), F32),
            pltpu.VMEM((STEPS + 1, 2, 8, T), F32),
            pltpu.VMEM((STEPS + 1, NY, 8, T), F32),
            pltpu.VMEM((STEPS + 1, NZ, 8, T), F32),
            dma((NP, NK + 1)),
            dma((NP, NK + 1)),
            pltpu.VMEM((2, NP, NX, PR, T), BF16),
            dma((3, NP)),
            dma((3, NP)),
            dma,
            dma((2 * NP, 2, NZ // 2)),
            dma((2 * NP, 2, NZ // 2)),
            dma((2 * NP, 2, NY // 2)),
            dma((2 * NP, 2, NY // 2)),
            dma((2 * NP, 2, NY // 2)),
            dma((2 * NP, 2, NY // 2)),
            dma((2 * NP, 2, NZ // 2)),
            dma((2 * NP, 2, NZ // 2)),
            dma((STEPS + 1, NY)),
            dma((STEPS + 1, NY)),
            dma((STEPS + 1, NZ)),
            dma((STEPS + 1, NZ)),
        ],
        compiler_params=pltpu.CompilerParams(
            collective_id=0, has_side_effects=True, vmem_limit_bytes=60 * 2**20
        ),
        cost_estimate=pl.CostEstimate(
            flops=STEPS * NS * 4 * T**3, bytes_accessed=4 * NS * T * T, transcendentals=0
        ),
        name="lanczos",
    )(
        start[0],
        left[0],
        right[0].reshape(NS, T, T),
        energy[0],
        rows[0],
        cols[0],
        order,
        goal,
        last,
        has,
    )
    return coef, residual[None]


def solution(mesh):
    return jax.shard_map(
        local,
        mesh=mesh,
        in_specs=(
            P("seg", "blk", None, None),
            P("seg", "blk", None, None, None),
            P("seg", "blk", None, None, None),
            P("seg", "blk"),
            P("seg", "blk"),
            P("seg", "blk"),
            P("seg", "blk", None),
        ),
        out_specs=(P("seg", None), P("seg", "blk", None, None)),
        check_vma=False,
    )
```
